32 devices in a mesh: groups: 2 (over y), fsdp: 4 (over z), tensor: 4 (over x, core).
Axes of the slice: x: 2, y: 2, z: 4, core: 2. Of those that a mesh axis runs over, the one named last changes fastest.
Arguments:
- hidden_states: bfloat16 [3072, 8192], P(('groups', 'fsdp'), 'tensor'), parts along dimension 0
- norm_gain: bfloat16 [8192], P('tensor'), may hold values from 0.099609375 to 1.8984375
- w_query: bfloat16 [8192, 4096], P('fsdp', 'tensor')
- w_keyval: bfloat16 [8192, 2, 1024], P('fsdp', None, 'tensor')
- segment_ids: int32 [8, 384], P(('groups', 'fsdp')), parts along dimension 0, may hold values from 0 to 7, never falling along the last dimension, each value on 1 to 192 neighbouring positions
Outputs:
- context: bfloat16 [3072, 4096], P(('groups', 'fsdp'), 'tensor'), parts along dimension 0
The draws below stay inside these ranges and needn't reach their ends.
There are 2 independent parts, one for each index of `groups`. The reference program is written for one: setup_inputs(seed, part) draws one part's arguments, and reference() takes and returns one part's arrays. A program takes and returns all parts, laid end to end along the dimension named above; an argument that names none is the same for every part. Nothing has to cross between parts.
Inputs may be any that keep to these rules, and one draw needn't show every extreme that they name: `segment_ids`: in each row the ids never fall; every rollout has 1 to 192 tokens and one has exactly 192.
All inputs are finite; a program needn't handle non-finite values.
Results may differ from the reference program's by a relative error of at most 0.012.
The reference program's roundings to bfloat16 on the way (of `normed`, `q_rot`, `k_rot`, `value` and `weights`) count: a program that leaves them out, or rounds other values in their place, can miss the bound.
Values may be sent and summed in bfloat16 or wider, within the bound.
No kernel may reach another device: no remote copies, remote signals or barrier semaphores. Data moves between devices by JAX's collectives and lax.ppermute only.
A program may use at most 128 MiB of HBM per device.

```python
import math
import jax
import jax.numpy as jnp
import numpy as np
from jax import lax

D = 8192
HEAD_DIM = 128
Q_HEADS = 32
KV_HEADS = 8
TOK_DEV = 384
SEG_COUNT = 8
SEG_MOST = 192
PACKS = 4
TOKENS = 1536
Q_COLS = 4096
KV_COLS = 1024


def key_base(key):
    return jax.random.normal(jax.random.fold_in(key, 101), (D, KV_COLS), jnp.float32)


def draw_hidden_states(key, part):
    key = jax.random.fold_in(key, 3)
    key_a, key_b, key_c = jax.random.split(key, 3)
    ramp = jnp.arange(D, dtype=jnp.float32) / D
    col_scale = jnp.exp(math.log(10.0) * ramp) * jax.random.uniform(key_b, (D,), jnp.float32, 0.7, 1.4)
    base = jax.random.normal(key_a, (TOKENS, D), jnp.float32)
    row_scale = jnp.exp(math.log(10.0) * jax.random.uniform(key_c, (TOKENS, 1), jnp.float32))
    return (0.1 * base * col_scale[None, :] * row_scale).astype(jnp.bfloat16)


def draw_w_keyval(key, part):
    base = key_base(key)
    key = jax.random.fold_in(key, 5)
    values = jax.random.normal(key, (D, KV_COLS), jnp.float32)
    return (jnp.stack((base, values), axis=1) * D ** (-0.5)).astype(jnp.bfloat16)


def draw_w_query(key, part):
    key = jax.random.fold_in(key, 7)
    key_a = jax.random.fold_in(key, 0)
    noise = jax.random.normal(key_a, (D, Q_COLS), jnp.float32)
    mixed = noise
    return (mixed * D ** (-0.5)).astype(jnp.bfloat16)


def length_profile(amount, total, most, lean):
    weights = [(1 << 20) // math.isqrt(standing ** lean) + 1 for standing in range(2, amount + 1)]
    rest, given = total - most - (amount - 1), [1] * (amount - 1)
    while rest > 0:
        free = [i for i in range(amount - 1) if given[i] < most]
        pool, remaining = sum([weights[i] for i in free]), rest
        for i in free:
            more = min(most - given[i], max(1, remaining * weights[i] // pool), rest)
            given[i] = given[i] + more
            rest = rest - more
    return np.array([most] + given)


def ragged(own_key, number_of, total, most, lean):
    if number_of == 2:
        one = jax.random.randint(own_key, (), max(1, total - most), min(most, total - 1) + 1)
        return jnp.stack([one, total - one])
    sizes = jnp.asarray(length_profile(number_of, total, most, lean), jnp.int32)
    twos = (number_of - 1) // 2
    giver, taker = sizes[1:1 + 2 * twos:2], sizes[2:2 + 2 * twos:2]
    margin = jnp.minimum(giver - 1, most - taker)
    shifted = jax.random.randint(jax.random.fold_in(own_key, 1), (twos,), 0, 1 << 20) % (margin + 1)
    sizes = sizes.at[1:1 + 2 * twos:2].set(giver - shifted).at[2:2 + 2 * twos:2].set(taker + shifted)
    return sizes[jax.random.permutation(jax.random.fold_in(own_key, 2), number_of)]


def setup_inputs(seed: int = 0, part: int = 0) -> dict:
    key_of = jax.random.split(jax.random.key(seed), 6)
    part_keys = jax.random.split(jax.random.fold_in(key_of[5], part), 6)
    hidden_states = draw_hidden_states(jax.random.fold_in(jax.random.fold_in(key_of[5], part), 71), part)
    norm_gain = jnp.clip(1.0 + 0.18 * jax.random.normal(key_of[1], (D,), jnp.float32), 0.099609375, 1.8984375).astype(jnp.bfloat16)
    w_query = draw_w_query(jax.random.fold_in(key_of[5], 71), part)
    w_keyval = draw_w_keyval(jax.random.fold_in(key_of[5], 71), part)
    segment_ids = jax.vmap(lambda own: jnp.searchsorted(jnp.cumsum(ragged(own, SEG_COUNT, TOK_DEV, SEG_MOST, 2)), jnp.arange(TOK_DEV), side="right"))(jax.random.split(part_keys[4], PACKS)).reshape((PACKS, TOK_DEV)).astype(jnp.int32)
    return {"hidden_states": hidden_states, "norm_gain": norm_gain, "w_query": w_query, "w_keyval": w_keyval, "segment_ids": segment_ids}


def positions(seg):
    length = seg.shape[0]
    index = jnp.arange(length, dtype=jnp.int32)
    change = jnp.concatenate((jnp.ones((1,), dtype=bool), seg[1:] != seg[:-1]))
    first = lax.cummax(jnp.where(change, index, jnp.int32(0)).astype(jnp.int32), axis=0)
    return (index - first).astype(jnp.int32)

def rope_tables(place, head_dim):
    half = head_dim // 2
    freq = jnp.exp(jnp.arange(half, dtype=jnp.float32) * (-2.0 * math.log(500000.0) / head_dim))
    angle = place.astype(jnp.float32)[:, None] * freq[None, :]
    return (jnp.cos(angle), jnp.sin(angle))

def rotate(vector, cosine, sine):
    half = vector.shape[-1] // 2
    first = vector[..., :half]
    second = vector[..., half:]
    cosine = cosine[:, None, :]
    sine = sine[:, None, :]
    return jnp.concatenate((first * cosine - second * sine, second * cosine + first * sine), axis=-1)

def attend_pack(query, key, value, seg):
    tlen = query.shape[0]
    hd = HEAD_DIM
    group = Q_HEADS // KV_HEADS
    place = positions(seg)
    cosine, sine = rope_tables(place, hd)
    q_rot = rotate(query.reshape(tlen, Q_HEADS, hd), cosine, sine).astype(jnp.bfloat16)
    k_rot = rotate(key.reshape(tlen, KV_HEADS, hd), cosine, sine).astype(jnp.bfloat16)
    v_val = value.reshape(tlen, KV_HEADS, hd).astype(jnp.bfloat16)
    grouped = q_rot.reshape(tlen, KV_HEADS, group, hd).astype(jnp.float32)
    scores = jnp.einsum('qkgd,skd->kgqs', grouped, k_rot.astype(jnp.float32)) * (1.0 / math.sqrt(hd))
    index = jnp.arange(tlen, dtype=jnp.int32)
    allowed = (seg[:, None] == seg[None, :]) & (index[None, :] <= index[:, None])
    scores = jnp.where(allowed[None, None], scores, -jnp.inf)
    top = lax.optimization_barrier(jnp.max(scores, axis=-1, keepdims=True))
    expo = jnp.exp(scores - top)
    weights = (expo / lax.optimization_barrier(jnp.sum(expo, axis=-1, keepdims=True))).astype(jnp.bfloat16)
    mixed = jnp.einsum('kgqs,skd->qkgd', weights.astype(jnp.float32), v_val.astype(jnp.float32))
    return mixed.astype(jnp.bfloat16).reshape(tlen, Q_COLS)

def reference(hidden_states, norm_gain, w_query, w_keyval, segment_ids):
    states = hidden_states.astype(jnp.float32)
    square_sum = lax.optimization_barrier(jnp.sum(states * states, axis=1, keepdims=True))
    scale = lax.rsqrt(square_sum / D + 1e-05)
    normed = (states * scale * norm_gain.astype(jnp.float32)[None, :]).astype(jnp.bfloat16)
    query = jnp.dot(normed, w_query, preferred_element_type=jnp.float32)
    keyval = jnp.dot(normed, w_keyval.reshape(D, 2 * KV_COLS), preferred_element_type=jnp.float32)

    def one_pack(items):
        q_pack, kv_pack, seg = items
        return attend_pack(q_pack, kv_pack[:, :KV_COLS], kv_pack[:, KV_COLS:], seg)
    packed = lax.map(one_pack, (query.reshape(PACKS, TOK_DEV, Q_COLS), keyval.reshape(PACKS, TOK_DEV, 2 * KV_COLS), segment_ids))
    return packed.reshape(TOKENS, Q_COLS)
```

```python
import math

import jax
import jax.numpy as jnp
from jax import lax
from jax.sharding import PartitionSpec as P

D = 8192
HEAD_DIM = 128
ORDER = ((3, 2, 1, 0), (3, 2, 0, 1), (0, 1, 3, 2), (0, 1, 2, 3))
PIECES = 1


def positions(seg):
    length = seg.shape[0]
    index = jnp.arange(length, dtype=jnp.int32)
    change = jnp.concatenate((jnp.ones((1,), dtype=bool), seg[1:] != seg[:-1]))
    first = lax.cummax(jnp.where(change, index, jnp.int32(0)), axis=0)
    return index - first


def rope_tables(place, head_dim):
    half = head_dim // 2
    freq = jnp.exp(jnp.arange(half, dtype=jnp.float32) * (-2.0 * math.log(500000.0) / head_dim))
    angle = place.astype(jnp.float32)[:, None] * freq[None, :]
    return (jnp.cos(angle), jnp.sin(angle))


def rotate(vector, cosine, sine):
    half = vector.shape[-1] // 2
    first = vector[..., :half]
    second = vector[..., half:]
    cosine = cosine[:, None, :]
    sine = sine[:, None, :]
    return jnp.concatenate(
        (first * cosine - second * sine, second * cosine + first * sine), axis=-1
    )


def rotated_keys(keyval, cosine, sine):
    tlen = keyval.shape[0]
    kv_local = keyval.shape[1] // 2
    kv_heads = kv_local // HEAD_DIM
    k_rot = rotate(keyval[:, :kv_local].reshape(tlen, kv_heads, HEAD_DIM), cosine, sine).astype(
        jnp.bfloat16
    )
    v_val = keyval[:, kv_local:].reshape(tlen, kv_heads, HEAD_DIM).astype(jnp.bfloat16)
    return (k_rot, v_val)


def attend(query, k_rot, v_val, seg, cosine, sine, start):
    tlen = query.shape[0]
    klen, kv_heads = k_rot.shape[:2]
    heads = query.shape[1] // HEAD_DIM
    group = heads // kv_heads
    rows = slice(start, start + tlen)
    q_rot = rotate(query.reshape(tlen, heads, HEAD_DIM), cosine[rows], sine[rows]).astype(jnp.bfloat16)
    grouped = q_rot.reshape(tlen, kv_heads, group, HEAD_DIM)
    scores = jnp.einsum("qkgd,skd->kgqs", grouped, k_rot, preferred_element_type=jnp.float32) * (
        1.0 / math.sqrt(HEAD_DIM)
    )
    index = jnp.arange(seg.shape[0], dtype=jnp.int32)
    allowed = (seg[rows, None] == seg[None, :klen]) & (index[None, :klen] <= index[rows, None])
    scores = jnp.where(allowed[None, None], scores, -jnp.inf)
    top = jnp.max(scores, axis=-1, keepdims=True)
    expo = jnp.exp(scores - top)
    weights = (expo / jnp.sum(expo, axis=-1, keepdims=True)).astype(jnp.bfloat16)
    mixed = jnp.einsum("kgqs,skd->qkgd", weights, v_val, preferred_element_type=jnp.float32)
    return mixed.astype(jnp.bfloat16).reshape(tlen, heads * HEAD_DIM)


def gathered(hidden_states, norm_gain, w_query, w_keyval, segment_ids):
    whole = lax.all_gather(hidden_states, "tensor", axis=1, tiled=True)
    gain_full = lax.all_gather(norm_gain, "tensor", axis=0, tiled=True)
    local_sq = jnp.sum(jnp.square(hidden_states.astype(jnp.float32)), axis=1, keepdims=True)
    scale = lax.rsqrt(lax.psum(local_sq, "tensor") / D + 1e-05)
    normed = (whole.astype(jnp.float32) * scale * gain_full.astype(jnp.float32)[None, :]).astype(
        jnp.bfloat16
    )
    w_rows = w_keyval.shape[0]
    kv_weight = w_keyval.reshape(w_rows, 2 * w_keyval.shape[2])
    seg = segment_ids[0]
    cosine, sine = rope_tables(positions(seg), HEAD_DIM)

    def add_rows(piece):
        return jnp.dot(normed, piece, preferred_element_type=jnp.float32)

    query = add_rows(lax.all_gather(w_query, "fsdp", axis=0, tiled=True))
    keyval = add_rows(lax.all_gather(kv_weight, "fsdp", axis=0, tiled=True))
    k_rot, v_val = rotated_keys(keyval, cosine, sine)
    return attend(query, k_rot, v_val, seg, cosine, sine, 0)


def partial_sums(hidden_states, norm_gain, w_query, w_keyval, segment_ids):
    z = lax.axis_index("fsdp")
    tokens = hidden_states.shape[0]
    half = tokens // 2
    size = half // PIECES
    both = ("fsdp", "tensor")
    q_cols = w_query.shape[1]

    def at(row, col):
        return row * 4 + col

    def over_z(stage, flip):
        return [(at(ORDER[j][stage], j ^ flip), at(j, j ^ flip)) for j in range(4)]

    def over_x(flip):
        return [(at(j, j ^ flip), at(j, j ^ flip ^ 2)) for j in range(4)]

    over_core = [(at(j, j ^ flip), at(j, j ^ flip ^ 1)) for j in range(4) for flip in (0, 2)]

    swap_x = [(t, t ^ 2) for t in range(4)]
    crossed = [
        lax.ppermute(hidden_states[half + n * size : half + (n + 1) * size], "tensor", swap_x)
        for n in range(PIECES)
    ]
    direct = [hidden_states[n * size : (n + 1) * size] for n in range(PIECES)]
    sources = [(piece, 0) for piece in direct] + [(piece, 2) for piece in crossed]

    local_sq = jnp.sum(jnp.square(hidden_states.astype(jnp.float32)), axis=1)
    squares = lax.all_gather(local_sq, both, axis=0, tiled=False).reshape(4, 4, tokens)
    scales = lax.rsqrt(jnp.sum(squares, axis=1) / D + 1e-05)
    gain = lax.ppermute(norm_gain, both, [(at(i, j), at(j, i)) for i in range(4) for j in range(4)])
    gain = gain.astype(jnp.float32)[None, :]

    weight = jnp.concatenate((w_query, w_keyval.reshape(w_keyval.shape[0], -1)), axis=1)
    seg = segment_ids[0]
    cosine, sine = rope_tables(positions(seg), HEAD_DIM)
    order = jnp.array(ORDER, dtype=jnp.int32)[z]

    def spread(piece, flip):
        other = lax.ppermute(piece, both, over_x(flip))
        mine = piece + other
        return mine + lax.ppermute(mine, both, over_core)

    def product(piece, stage, n):
        scale = lax.dynamic_slice(scales, (order[stage], n * size), (1, size))[0]
        normed = (piece.astype(jnp.float32) * scale[:, None] * gain).astype(jnp.bfloat16)
        return jnp.dot(normed, weight, preferred_element_type=jnp.float32)

    own_block = jnp.where(lax.axis_index("tensor") == z, hidden_states, jnp.zeros_like(hidden_states))
    own_block = spread(own_block, 0)
    outer_in = [(0, 1), (3, 2)]
    sums = []
    for n, (piece, flip) in enumerate(sources):
        first, second, third = (
            product(spread(lax.ppermute(piece, both, over_z(stage, flip)), flip), stage, n).astype(
                jnp.bfloat16
            )
            for stage in range(3)
        )
        from_far = lax.ppermute(first, "fsdp", outer_in) + first
        from_mid = lax.ppermute(second, "fsdp", outer_in) + second
        near = lax.ppermute(third, "fsdp", [(0, 1), (1, 0), (2, 3), (3, 2)])
        far = lax.ppermute(from_far, "fsdp", [(1, 3), (2, 0)])
        mid = lax.ppermute(from_mid, "fsdp", [(1, 2), (2, 1)])
        own = product(own_block[n * size : (n + 1) * size], 3, n)
        sums.append(
            own + near.astype(jnp.float32) + far.astype(jnp.float32) + mid.astype(jnp.float32)
        )

    outs = []
    keys, values = [], []
    for n, total in enumerate(sums):
        rows = slice(n * size, (n + 1) * size)
        k_rot, v_val = rotated_keys(total[:, q_cols:], cosine[rows], sine[rows])
        keys.append(k_rot)
        values.append(v_val)
        outs.append(
            attend(
                total[:, :q_cols],
                jnp.concatenate(keys),
                jnp.concatenate(values),
                seg,
                cosine,
                sine,
                n * size,
            )
        )
    return jnp.concatenate(outs)


def solution(mesh):
    in_specs = (
        P(("groups", "fsdp"), "tensor"),
        P("tensor"),
        P("fsdp", "tensor"),
        P("fsdp", None, "tensor"),
        P(("groups", "fsdp"), None),
    )
    out_specs = P(("groups", "fsdp"), "tensor")
    square = mesh.shape["fsdp"] == 4 and mesh.shape["tensor"] == 4
    step = partial_sums if square else gathered
    return jax.shard_map(step, mesh=mesh, in_specs=in_specs, out_specs=out_specs, check_vma=False)
```

```python
import math

import jax
import jax.numpy as jnp
from jax import lax
from jax.sharding import PartitionSpec as P

D = 8192
HEAD_DIM = 128
ORDER = ((3, 2, 1, 0), (3, 2, 0, 1), (0, 1, 3, 2), (0, 1, 2, 3))
SIZES = (48, 48, 48, 48)
TURNS = "s0 w s1 x0 s2 c0 x1 s3 m0 c1 x2 m1 c2 x3 m2 c3 f0 m3 f1 f2 f3"


def positions(seg):
    length = seg.shape[0]
    index = jnp.arange(length, dtype=jnp.int32)
    change = jnp.concatenate((jnp.ones((1,), dtype=bool), seg[1:] != seg[:-1]))
    first = lax.cummax(jnp.where(change, index, jnp.int32(0)), axis=0)
    return index - first


def rope_tables(place, head_dim):
    half = head_dim // 2
    freq = jnp.exp(jnp.arange(half, dtype=jnp.float32) * (-2.0 * math.log(500000.0) / head_dim))
    angle = place.astype(jnp.float32)[:, None] * freq[None, :]
    return (jnp.cos(angle), jnp.sin(angle))


def rotate(vector, cosine, sine):
    half = vector.shape[-1] // 2
    first = vector[..., :half]
    second = vector[..., half:]
    cosine = cosine[:, None, :]
    sine = sine[:, None, :]
    return jnp.concatenate(
        (first * cosine - second * sine, second * cosine + first * sine), axis=-1
    )


def rotated_keys(keyval, cosine, sine):
    tlen = keyval.shape[0]
    kv_local = keyval.shape[1] // 2
    kv_heads = kv_local // HEAD_DIM
    k_rot = rotate(keyval[:, :kv_local].reshape(tlen, kv_heads, HEAD_DIM), cosine, sine).astype(
        jnp.bfloat16
    )
    v_val = keyval[:, kv_local:].reshape(tlen, kv_heads, HEAD_DIM).astype(jnp.bfloat16)
    return (k_rot, v_val)


def attend(query, k_rot, v_val, seg, cosine, sine, start):
    tlen = query.shape[0]
    klen, kv_heads = k_rot.shape[:2]
    heads = query.shape[1] // HEAD_DIM
    group = heads // kv_heads
    rows = slice(start, start + tlen)
    q_rot = rotate(query.reshape(tlen, heads, HEAD_DIM), cosine[rows], sine[rows]).astype(jnp.bfloat16)
    grouped = q_rot.reshape(tlen, kv_heads, group, HEAD_DIM)
    scores = jnp.einsum("qkgd,skd->kgqs", grouped, k_rot, preferred_element_type=jnp.float32) * (
        1.0 / math.sqrt(HEAD_DIM)
    )
    index = jnp.arange(seg.shape[0], dtype=jnp.int32)
    allowed = (seg[rows, None] == seg[None, :klen]) & (index[None, :klen] <= index[rows, None])
    scores = jnp.where(allowed[None, None], scores, -jnp.inf)
    top = jnp.max(scores, axis=-1, keepdims=True)
    expo = jnp.exp(scores - top)
    weights = (expo / jnp.sum(expo, axis=-1, keepdims=True)).astype(jnp.bfloat16)
    mixed = jnp.einsum("kgqs,skd->qkgd", weights, v_val, preferred_element_type=jnp.float32)
    return mixed.astype(jnp.bfloat16).reshape(tlen, heads * HEAD_DIM)


def gathered(hidden_states, norm_gain, w_query, w_keyval, segment_ids):
    whole = lax.all_gather(hidden_states, "tensor", axis=1, tiled=True)
    gain_full = lax.all_gather(norm_gain, "tensor", axis=0, tiled=True)
    local_sq = jnp.sum(jnp.square(hidden_states.astype(jnp.float32)), axis=1, keepdims=True)
    scale = lax.rsqrt(lax.psum(local_sq, "tensor") / D + 1e-05)
    normed = (whole.astype(jnp.float32) * scale * gain_full.astype(jnp.float32)[None, :]).astype(
        jnp.bfloat16
    )
    w_rows = w_keyval.shape[0]
    kv_weight = w_keyval.reshape(w_rows, 2 * w_keyval.shape[2])
    seg = segment_ids[0]
    cosine, sine = rope_tables(positions(seg), HEAD_DIM)

    def add_rows(piece):
        return jnp.dot(normed, piece, preferred_element_type=jnp.float32)

    query = add_rows(lax.all_gather(w_query, "fsdp", axis=0, tiled=True))
    keyval = add_rows(lax.all_gather(kv_weight, "fsdp", axis=0, tiled=True))
    k_rot, v_val = rotated_keys(keyval, cosine, sine)
    return attend(query, k_rot, v_val, seg, cosine, sine, 0)


def partial_sums(hidden_states, norm_gain, w_query, w_keyval, segment_ids):
    z = lax.axis_index("fsdp")
    t = lax.axis_index("tensor")
    tokens = hidden_states.shape[0]
    both = ("fsdp", "tensor")
    q_cols = w_query.shape[1]

    def toward(far):
        pairs = []
        for i in range(4):
            for col in range(4):
                j = col if (col // 2 != i // 2) == far else col ^ 2
                pairs.append((i * 4 + col, j * 4 + col // 2 * 2 + ORDER[j].index(i) % 2))
        return pairs

    swap_x = [(n, n ^ 2) for n in range(4)]
    swap_core = [(n, n ^ 1) for n in range(4)]
    outer_in = [(0, 1), (3, 2)]
    count = len(SIZES)

    starts = [sum(SIZES[:n]) * 2 for n in range(count)]
    crossed = [
        lax.ppermute(hidden_states[start + size : start + 2 * size], "tensor", swap_x)
        for start, size in zip(starts, SIZES)
    ]
    local_sq = jnp.sum(jnp.square(hidden_states.astype(jnp.float32)), axis=1)
    square_sum = local_sq
    for flip in (1, 2, 3):
        square_sum += lax.ppermute(local_sq, "tensor", [(n, n ^ flip) for n in range(4)])
    scale = lax.rsqrt(square_sum / D + 1e-05)[:, None]
    gain = norm_gain.astype(jnp.float32)[None, :]
    crossed_gain = lax.ppermute(norm_gain, "tensor", swap_x).astype(jnp.float32)[None, :]

    here_far = t // 2 != z // 2
    even_core = t % 2 == 0
    done = [scale]

    def in_turn(*arrays):
        arrays, _ = lax.optimization_barrier((arrays, done[0]))
        return arrays

    state = [{} for _ in SIZES]

    def send(n):
        start, size = starts[n], SIZES[n]
        mid = start + size
        stay, other = in_turn(hidden_states[start:mid], crossed[n])
        stay = (stay.astype(jnp.float32) * scale[start:mid] * gain).astype(jnp.bfloat16)
        other = other.astype(jnp.float32) * scale[mid : mid + size] * crossed_gain
        other = other.astype(jnp.bfloat16)
        far = jnp.where(here_far, stay, other)
        near = jnp.where(here_far, other, stay)
        done[0] = (far, near)
        state[n]["z"] = lax.ppermute(far, both, toward(True)), lax.ppermute(near, both, toward(False))

    def cross(n):
        mine = jnp.stack(in_turn(*state[n]["z"]))
        done[0] = mine
        state[n]["x"] = mine, lax.ppermute(mine, "tensor", swap_x)

    def share(n):
        mine, theirs = in_turn(*state[n]["x"])
        mine = jnp.where(
            here_far, jnp.concatenate((theirs, mine), 1), jnp.concatenate((mine, theirs), 1)
        )
        done[0] = mine
        state[n]["c"] = mine, lax.ppermute(mine, "tensor", swap_core)

    def multiply(n):
        mine, theirs = in_turn(*state[n]["c"])
        rows = jnp.where(
            even_core, jnp.stack((mine, theirs), 1), jnp.stack((theirs, mine), 1)
        ).reshape(8 * SIZES[n], -1)
        part = jnp.dot(rows, weight, preferred_element_type=jnp.float32)
        part = part.reshape(4, 2 * SIZES[n], -1)
        outer = part[:2].astype(jnp.bfloat16)
        inner = part[2].astype(jnp.bfloat16)
        done[0] = (outer, inner)
        passed = lax.ppermute(outer, "fsdp", outer_in)
        near_sum = lax.ppermute(inner, "fsdp", [(0, 1), (1, 0), (2, 3), (3, 2)])
        state[n]["p"] = part[3], outer, passed, near_sum

    def forward(n):
        own, outer, passed, near_sum = state[n]["p"]
        passed, outer = in_turn(passed, outer)
        passed = passed + outer
        done[0] = passed
        far_sum = lax.ppermute(passed[0], "fsdp", [(1, 3), (2, 0)])
        mid_sum = lax.ppermute(passed[1], "fsdp", [(1, 2), (2, 1)])
        state[n]["f"] = own, near_sum, far_sum, mid_sum

    def finish(n):
        own, near_sum, far_sum, mid_sum = state[n]["f"]
        return (
            own
            + near_sum.astype(jnp.float32)
            + far_sum.astype(jnp.float32)
            + mid_sum.astype(jnp.float32)
        )

    steps = {"s": send, "x": cross, "c": share, "m": multiply, "f": forward}
    for turn in TURNS.split():
        if turn == "w":
            w_query, w_keyval = in_turn(w_query, w_keyval)
            weight = jnp.concatenate((w_query, w_keyval.reshape(w_keyval.shape[0], -1)), axis=1)
            done[0] = weight
        else:
            steps[turn[0]](int(turn[1]))

    seg = segment_ids[0]
    cosine, sine = rope_tables(positions(seg), HEAD_DIM)
    total = jnp.concatenate([finish(n) for n in range(count)])
    k_rot, v_val = rotated_keys(total[:, q_cols:], cosine, sine)
    return attend(total[:, :q_cols], k_rot, v_val, seg, cosine, sine, 0)


def solution(mesh):
    in_specs = (
        P(("groups", "fsdp"), "tensor"),
        P("tensor"),
        P("fsdp", "tensor"),
        P("fsdp", None, "tensor"),
        P(("groups", "fsdp"), None),
    )
    out_specs = P(("groups", "fsdp"), "tensor")
    square = mesh.shape["fsdp"] == 4 and mesh.shape["tensor"] == 4
    step = partial_sums if square else gathered
    return jax.shard_map(step, mesh=mesh, in_specs=in_specs, out_specs=out_specs, check_vma=False)
```

```python
import functools
import math

import jax
import jax.numpy as jnp
from jax import lax
from jax.experimental import pallas as pl
from jax.experimental.pallas import tpu as pltpu
from jax.sharding import PartitionSpec as P

D = 8192
HEAD_DIM = 128
ORDER = ((3, 2, 1, 0), (3, 2, 0, 1), (0, 1, 3, 2), (0, 1, 2, 3))
SIZES = (48, 48, 48, 48)
PIECES = ((0, 0, 96), (1, 0, 96), (2, 0, 96), (3, 0, 96))
TURNS = (
    "a0",
    "a1",
    "n",
    "s0",
    "a2",
    "s1",
    "x0",
    "w",
    "a3",
    "s2",
    "x1",
    "c0",
    "s3",
    "x2",
    "c1",
    "m0",
    "x3",
    "c2",
    "m1",
    "f0",
    "c3",
    "m2",
    "f1",
    "d0",
    "m3",
    "f2",
    "d1",
    "f3",
    "d2",
    "d3",
)


def positions(seg):
    length = seg.shape[0]
    index = jnp.arange(length, dtype=jnp.int32)
    change = jnp.concatenate((jnp.ones((1,), dtype=bool), seg[1:] != seg[:-1]))
    first = lax.cummax(jnp.where(change, index, jnp.int32(0)), axis=0)
    return index - first


def rope_tables(place, head_dim):
    half = head_dim // 2
    freq = jnp.exp(jnp.arange(half, dtype=jnp.float32) * (-2.0 * math.log(500000.0) / head_dim))
    angle = place.astype(jnp.float32)[:, None] * freq[None, :]
    return (jnp.cos(angle), jnp.sin(angle))


def rotate(vector, cosine, sine):
    half = vector.shape[-1] // 2
    first = vector[..., :half]
    second = vector[..., half:]
    cosine = cosine[:, None, :]
    sine = sine[:, None, :]
    return jnp.concatenate(
        (first * cosine - second * sine, second * cosine + first * sine), axis=-1
    )


def rotated_keys(keyval, cosine, sine):
    tlen = keyval.shape[0]
    kv_local = keyval.shape[1] // 2
    kv_heads = kv_local // HEAD_DIM
    k_rot = rotate(keyval[:, :kv_local].reshape(tlen, kv_heads, HEAD_DIM), cosine, sine).astype(
        jnp.bfloat16
    )
    v_val = keyval[:, kv_local:].reshape(tlen, kv_heads, HEAD_DIM).astype(jnp.bfloat16)
    return (k_rot, v_val)


def attend(query, k_rot, v_val, seg, cosine, sine, start):
    tlen = query.shape[0]
    klen, kv_heads = k_rot.shape[:2]
    heads = query.shape[1] // HEAD_DIM
    group = heads // kv_heads
    rows = slice(start, start + tlen)
    q_rot = rotate(query.reshape(tlen, heads, HEAD_DIM), cosine[rows], sine[rows]).astype(jnp.bfloat16)
    grouped = q_rot.reshape(tlen, kv_heads, group, HEAD_DIM)
    scores = jnp.einsum("qkgd,skd->kgqs", grouped, k_rot, preferred_element_type=jnp.float32) * (
        1.0 / math.sqrt(HEAD_DIM)
    )
    index = jnp.arange(seg.shape[0], dtype=jnp.int32)
    allowed = (seg[rows, None] == seg[None, :klen]) & (index[None, :klen] <= index[rows, None])
    scores = jnp.where(allowed[None, None], scores, -jnp.inf)
    top = jnp.max(scores, axis=-1, keepdims=True)
    expo = jnp.exp(scores - top)
    weights = (expo / jnp.sum(expo, axis=-1, keepdims=True)).astype(jnp.bfloat16)
    mixed = jnp.einsum("kgqs,skd->qkgd", weights, v_val, preferred_element_type=jnp.float32)
    return mixed.astype(jnp.bfloat16).reshape(tlen, heads * HEAD_DIM)


def gathered(hidden_states, norm_gain, w_query, w_keyval, segment_ids):
    whole = lax.all_gather(hidden_states, "tensor", axis=1, tiled=True)
    gain_full = lax.all_gather(norm_gain, "tensor", axis=0, tiled=True)
    local_sq = jnp.sum(jnp.square(hidden_states.astype(jnp.float32)), axis=1, keepdims=True)
    scale = lax.rsqrt(lax.psum(local_sq, "tensor") / D + 1e-05)
    normed = (whole.astype(jnp.float32) * scale * gain_full.astype(jnp.float32)[None, :]).astype(
        jnp.bfloat16
    )
    w_rows = w_keyval.shape[0]
    kv_weight = w_keyval.reshape(w_rows, 2 * w_keyval.shape[2])
    seg = segment_ids[0]
    cosine, sine = rope_tables(positions(seg), HEAD_DIM)

    def add_rows(piece):
        return jnp.dot(normed, piece, preferred_element_type=jnp.float32)

    query = add_rows(lax.all_gather(w_query, "fsdp", axis=0, tiled=True))
    keyval = add_rows(lax.all_gather(kv_weight, "fsdp", axis=0, tiled=True))
    k_rot, v_val = rotated_keys(keyval, cosine, sine)
    return attend(query, k_rot, v_val, seg, cosine, sine, 0)


def attend_kernel(start, *refs):
    own_ref, near_ref, far_ref, mid_ref, cos_ref, sin_ref, column_ref, row_ref, *refs = refs
    if start:
        old_ref, _, out_ref, kv_ref, held, sem = refs
        kv_ref[...] = old_ref[...]
    else:
        out_ref, kv_ref, held, sem = refs
        kv_ref[...] = jnp.zeros_like(kv_ref)
    size = own_ref.shape[0]
    q_cols = held.shape[1]
    kv_cols = kv_ref.shape[2]
    group = q_cols // kv_cols
    rows = slice(start, start + size)
    seen = min(-(-(start + size) // HEAD_DIM) * HEAD_DIM, kv_ref.shape[1])
    cosine, sine = cos_ref[rows, :], sin_ref[rows, :]

    def total(col):
        cols = slice(col, col + HEAD_DIM)
        return (
            own_ref[:, cols]
            + near_ref[:, cols].astype(jnp.float32)
            + far_ref[:, cols].astype(jnp.float32)
            + mid_ref[:, cols].astype(jnp.float32)
        )

    def rotated(col):
        head = total(col)
        return (head * cosine + pltpu.roll(head, HEAD_DIM // 2, 1) * sine).astype(jnp.bfloat16)

    for col in range(0, kv_cols, HEAD_DIM):
        kv_ref[0, rows, col : col + HEAD_DIM] = rotated(q_cols + col)
        kv_ref[1, rows, col : col + HEAD_DIM] = total(q_cols + kv_cols + col).astype(jnp.bfloat16)
    shape = (size, seen)
    later = lax.broadcasted_iota(jnp.int32, shape, 1) > lax.broadcasted_iota(jnp.int32, shape, 0) + start
    allowed = jnp.logical_and(column_ref[rows, :] == row_ref[:, :seen], jnp.logical_not(later))
    bias = jnp.where(allowed, 0.0, -jnp.inf)
    bias = jnp.concatenate([bias] * group)
    for head in range(kv_cols // HEAD_DIM):
        cols = slice(head * HEAD_DIM, (head + 1) * HEAD_DIM)
        base = head * group * HEAD_DIM
        queries = jnp.concatenate([rotated(base + g * HEAD_DIM) for g in range(group)])
        scores = lax.dot_general(
            queries,
            kv_ref[0, :seen, cols],
            (((1,), (1,)), ((), ())),
            preferred_element_type=jnp.float32,
        )
        scores = scores * (1.0 / math.sqrt(HEAD_DIM)) + bias
        expo = jnp.exp(scores - jnp.max(scores, axis=1, keepdims=True))
        weights = (expo * (1.0 / jnp.sum(expo, axis=1, keepdims=True))).astype(jnp.bfloat16)
        mixed = jnp.dot(weights, kv_ref[1, :seen, cols], preferred_element_type=jnp.float32)
        for g in range(group):
            held[:, base + g * HEAD_DIM : base + (g + 1) * HEAD_DIM] = mixed[
                g * size : (g + 1) * size
            ].astype(jnp.bfloat16)
    copy = pltpu.make_async_copy(held, out_ref.at[pl.ds(start, size)], sem)
    copy.start()
    copy.wait()


def attend_piece(start, sums, tables, before, tokens, q_cols):
    size, cols = sums[0].shape
    kv = jax.ShapeDtypeStruct((2, tokens, (cols - q_cols) // 2), jnp.bfloat16)
    out = jax.ShapeDtypeStruct((tokens, q_cols), jnp.bfloat16)
    here = pl.BlockSpec(memory_space=pltpu.VMEM)
    anywhere = pl.BlockSpec(memory_space=pl.ANY)
    return pl.pallas_call(
        functools.partial(attend_kernel, start),
        in_specs=[here] * 8 + ([here, anywhere] if start else []),
        out_specs=[anywhere, here],
        out_shape=[out, kv],
        scratch_shapes=[pltpu.VMEM((size, q_cols), jnp.bfloat16), pltpu.SemaphoreType.DMA],
        input_output_aliases={9: 0} if start else {},
        compiler_params=pltpu.CompilerParams(vmem_limit_bytes=24 * 2**20),
        cost_estimate=pl.CostEstimate(flops=0, bytes_accessed=0, transcendentals=0),
    )(*sums, *tables, *before)


def partial_sums(hidden_states, norm_gain, w_query, w_keyval, segment_ids):
    z = lax.axis_index("fsdp")
    t = lax.axis_index("tensor")
    tokens = hidden_states.shape[0]
    both = ("fsdp", "tensor")
    q_cols = w_query.shape[1]

    def toward(far):
        pairs = []
        for i in range(4):
            for col in range(4):
                j = col if (col // 2 != i // 2) == far else col ^ 2
                pairs.append((i * 4 + col, j * 4 + col // 2 * 2 + ORDER[j].index(i) % 2))
        return pairs

    swap_x = [(n, n ^ 2) for n in range(4)]
    swap_core = [(n, n ^ 1) for n in range(4)]
    outer_in = [(0, 1), (3, 2)]
    count = len(SIZES)

    starts = [sum(SIZES[:n]) * 2 for n in range(count)]
    local_sq = jnp.sum(jnp.square(hidden_states.astype(jnp.float32)), axis=1)
    gain = norm_gain.astype(jnp.float32)
    squares = [
        lax.ppermute(local_sq, "tensor", [(n, n ^ flip) for n in range(4)]) for flip in (1, 3)
    ]
    partner = lax.ppermute(jnp.concatenate((local_sq, gain)), "tensor", swap_x)
    crossed_gain = partner[None, tokens:]
    gain = gain[None, :]

    here_far = t // 2 != z // 2
    even_core = t % 2 == 0
    done = [local_sq]

    def in_turn(*arrays):
        arrays, _ = lax.optimization_barrier((arrays, done[0]))
        return arrays

    state = [{} for _ in SIZES]
    sums = [{} for _ in PIECES]
    before = ()

    def across(n):
        start, size = starts[n], SIZES[n]
        piece = hidden_states[start + size : start + 2 * size]
        if n:
            (piece,) = in_turn(piece)
            done[0] = piece
        state[n]["a"] = lax.ppermute(piece, "tensor", swap_x)

    def send(n):
        start, size = starts[n], SIZES[n]
        mid = start + size
        stay, other = in_turn(hidden_states[start:mid], state[n]["a"])
        stay = (stay.astype(jnp.float32) * scale[start:mid] * gain).astype(jnp.bfloat16)
        other = other.astype(jnp.float32) * scale[mid : mid + size] * crossed_gain
        other = other.astype(jnp.bfloat16)
        far = jnp.where(here_far, stay, other)
        near = jnp.where(here_far, other, stay)
        done[0] = (far, near)
        state[n]["z"] = lax.ppermute(far, both, toward(True)), lax.ppermute(near, both, toward(False))

    def cross(n):
        mine = jnp.stack(in_turn(*state[n]["z"]))
        done[0] = mine
        state[n]["x"] = mine, lax.ppermute(mine, "tensor", swap_x)

    def share(n):
        mine, theirs = in_turn(*state[n]["x"])
        mine = jnp.where(
            here_far, jnp.concatenate((theirs, mine), 1), jnp.concatenate((mine, theirs), 1)
        )
        done[0] = mine
        state[n]["c"] = mine, lax.ppermute(mine, "tensor", swap_core)

    def multiply(n):
        batch, begin, end = PIECES[n]
        mine, theirs = in_turn(*(array[:, begin:end] for array in state[batch]["c"]))
        rows = jnp.where(even_core, jnp.stack((mine, theirs), 1), jnp.stack((theirs, mine), 1))
        rows = rows.reshape(4 * (end - begin), -1)
        part = jnp.dot(rows, weight, preferred_element_type=jnp.float32)
        part = part.reshape(4, end - begin, -1)
        outer = part[:2].astype(jnp.bfloat16)
        inner = part[2].astype(jnp.bfloat16)
        done[0] = (outer, inner)
        passed = lax.ppermute(outer, "fsdp", outer_in)
        near_sum = lax.ppermute(inner, "fsdp", [(0, 1), (1, 0), (2, 3), (3, 2)])
        sums[n]["p"] = part[3], outer, passed, near_sum

    def forward(n):
        own, outer, passed, near_sum = sums[n]["p"]
        passed, outer = in_turn(passed, outer)
        passed = passed + outer
        done[0] = passed
        far_sum = lax.ppermute(passed[0], "fsdp", [(1, 3), (2, 0)])
        mid_sum = lax.ppermute(passed[1], "fsdp", [(1, 2), (2, 1)])
        sums[n]["f"] = own, near_sum, far_sum, mid_sum

    def finish(n):
        batch, begin, _ = PIECES[n]
        added = in_turn(*sums[n]["f"])
        out, kv = attend_piece(starts[batch] + begin, added, tables, before, tokens, q_cols)
        done[0] = kv
        return kv, out

    seg = segment_ids[0]
    cosine, sine = rope_tables(positions(seg), HEAD_DIM)
    tables = (
        jnp.concatenate((cosine, cosine), 1),
        jnp.concatenate((-sine, sine), 1),
        seg[:, None],
        seg[None, :],
    )
    steps = {"a": across, "s": send, "x": cross, "c": share, "m": multiply, "f": forward}
    for turn in TURNS:
        if turn == "n":
            *received, state[0]["a"] = in_turn(partner[:tokens], *squares, state[0]["a"])
            done[0] = scale = lax.rsqrt((local_sq + sum(received)) / D + 1e-05)[:, None]
        elif turn == "w":
            w_query, w_keyval = in_turn(w_query, w_keyval)
            weight = jnp.concatenate((w_query, w_keyval.reshape(w_keyval.shape[0], -1)), axis=1)
            done[0] = weight
        elif turn[0] == "d":
            before = finish(int(turn[1]))
        else:
            steps[turn[0]](int(turn[1]))

    return before[1]


def solution(mesh):
    in_specs = (
        P(("groups", "fsdp"), "tensor"),
        P("tensor"),
        P("fsdp", "tensor"),
        P("fsdp", None, "tensor"),
        P(("groups", "fsdp"), None),
    )
    out_specs = P(("groups", "fsdp"), "tensor")
    square = mesh.shape["fsdp"] == 4 and mesh.shape["tensor"] == 4
    step = partial_sums if square else gathered
    return jax.shard_map(step, mesh=mesh, in_specs=in_specs, out_specs=out_specs, check_vma=False)
```

```python
import functools
import math

import jax
import jax.numpy as jnp
from jax import lax
from jax.experimental import pallas as pl
from jax.experimental.pallas import tpu as pltpu
from jax.sharding import PartitionSpec as P

D = 8192
HEAD_DIM = 128
ORDER = ((3, 2, 1, 0), (3, 2, 0, 1), (0, 1, 3, 2), (0, 1, 2, 3))
SIZES = (48, 48, 48, 48)
JOINT = (0, 1, 2, 3)
TURNS = (
    "a0",
    "n",
    "s0",
    "z0",
    "a1",
    "a2",
    "s1",
    "z1",
    "x0",
    "s2",
    "a3",
    "z2",
    "x1",
    "s3",
    "c0",
    "z3",
    "x2",
    "w",
    "c1",
    "m0",
    "k0",
    "x3",
    "c2",
    "m1",
    "e0",
    "k1",
    "f0",
    "c3",
    "m2",
    "e1",
    "k2",
    "f1",
    "d0",
    "m3",
    "k3",
    "e2",
    "f2",
    "d1",
    "e3",
    "f3",
    "d2",
    "d3",
)


def positions(seg):
    length = seg.shape[0]
    index = jnp.arange(length, dtype=jnp.int32)
    change = jnp.concatenate((jnp.ones((1,), dtype=bool), seg[1:] != seg[:-1]))
    first = lax.cummax(jnp.where(change, index, jnp.int32(0)), axis=0)
    return index - first


def rope_tables(place, head_dim):
    half = head_dim // 2
    freq = jnp.exp(jnp.arange(half, dtype=jnp.float32) * (-2.0 * math.log(500000.0) / head_dim))
    angle = place.astype(jnp.float32)[:, None] * freq[None, :]
    return (jnp.cos(angle), jnp.sin(angle))


def rotate(vector, cosine, sine):
    half = vector.shape[-1] // 2
    first = vector[..., :half]
    second = vector[..., half:]
    cosine = cosine[:, None, :]
    sine = sine[:, None, :]
    return jnp.concatenate(
        (first * cosine - second * sine, second * cosine + first * sine), axis=-1
    )


def rotated_keys(keyval, cosine, sine):
    tlen = keyval.shape[0]
    kv_local = keyval.shape[1] // 2
    kv_heads = kv_local // HEAD_DIM
    k_rot = rotate(keyval[:, :kv_local].reshape(tlen, kv_heads, HEAD_DIM), cosine, sine).astype(
        jnp.bfloat16
    )
    v_val = keyval[:, kv_local:].reshape(tlen, kv_heads, HEAD_DIM).astype(jnp.bfloat16)
    return (k_rot, v_val)


def attend(query, k_rot, v_val, seg, cosine, sine, start):
    tlen = query.shape[0]
    klen, kv_heads = k_rot.shape[:2]
    heads = query.shape[1] // HEAD_DIM
    group = heads // kv_heads
    rows = slice(start, start + tlen)
    q_rot = rotate(query.reshape(tlen, heads, HEAD_DIM), cosine[rows], sine[rows]).astype(jnp.bfloat16)
    grouped = q_rot.reshape(tlen, kv_heads, group, HEAD_DIM)
    scores = jnp.einsum("qkgd,skd->kgqs", grouped, k_rot, preferred_element_type=jnp.float32) * (
        1.0 / math.sqrt(HEAD_DIM)
    )
    index = jnp.arange(seg.shape[0], dtype=jnp.int32)
    allowed = (seg[rows, None] == seg[None, :klen]) & (index[None, :klen] <= index[rows, None])
    scores = jnp.where(allowed[None, None], scores, -jnp.inf)
    top = jnp.max(scores, axis=-1, keepdims=True)
    expo = jnp.exp(scores - top)
    weights = (expo / jnp.sum(expo, axis=-1, keepdims=True)).astype(jnp.bfloat16)
    mixed = jnp.einsum("kgqs,skd->qkgd", weights, v_val, preferred_element_type=jnp.float32)
    return mixed.astype(jnp.bfloat16).reshape(tlen, heads * HEAD_DIM)


def gathered(hidden_states, norm_gain, w_query, w_keyval, segment_ids):
    whole = lax.all_gather(hidden_states, "tensor", axis=1, tiled=True)
    gain_full = lax.all_gather(norm_gain, "tensor", axis=0, tiled=True)
    local_sq = jnp.sum(jnp.square(hidden_states.astype(jnp.float32)), axis=1, keepdims=True)
    scale = lax.rsqrt(lax.psum(local_sq, "tensor") / D + 1e-05)
    normed = (whole.astype(jnp.float32) * scale * gain_full.astype(jnp.float32)[None, :]).astype(
        jnp.bfloat16
    )
    w_rows = w_keyval.shape[0]
    kv_weight = w_keyval.reshape(w_rows, 2 * w_keyval.shape[2])
    seg = segment_ids[0]
    cosine, sine = rope_tables(positions(seg), HEAD_DIM)

    def add_rows(piece):
        return jnp.dot(normed, piece, preferred_element_type=jnp.float32)

    query = add_rows(lax.all_gather(w_query, "fsdp", axis=0, tiled=True))
    keyval = add_rows(lax.all_gather(kv_weight, "fsdp", axis=0, tiled=True))
    k_rot, v_val = rotated_keys(keyval, cosine, sine)
    return attend(query, k_rot, v_val, seg, cosine, sine, 0)


def attend_kernel(start, *refs):
    own_ref, near_ref, far_ref, mid_ref, cos_ref, sin_ref, column_ref, row_ref, *refs = refs
    if start:
        old_ref, _, out_ref, kv_ref, held, sem = refs
        kv_ref[...] = old_ref[...]
    else:
        out_ref, kv_ref, held, sem = refs
        kv_ref[...] = jnp.zeros_like(kv_ref)
    size = own_ref.shape[0]
    q_cols = held.shape[1]
    kv_cols = kv_ref.shape[2]
    group = q_cols // kv_cols
    rows = slice(start, start + size)
    seen = min(-(-(start + size) // HEAD_DIM) * HEAD_DIM, kv_ref.shape[1])
    cosine, sine = cos_ref[rows, :], sin_ref[rows, :]

    def total(col):
        cols = slice(col, col + HEAD_DIM)
        return (
            own_ref[:, cols]
            + near_ref[:, cols].astype(jnp.float32)
            + far_ref[:, cols].astype(jnp.float32)
            + mid_ref[:, cols].astype(jnp.float32)
        )

    def rotated(col):
        head = total(col)
        return (head * cosine + pltpu.roll(head, HEAD_DIM // 2, 1) * sine).astype(jnp.bfloat16)

    for col in range(0, kv_cols, HEAD_DIM):
        kv_ref[0, rows, col : col + HEAD_DIM] = rotated(q_cols + col)
        kv_ref[1, rows, col : col + HEAD_DIM] = total(q_cols + kv_cols + col).astype(jnp.bfloat16)
    shape = (size, seen)
    later = lax.broadcasted_iota(jnp.int32, shape, 1) > lax.broadcasted_iota(jnp.int32, shape, 0) + start
    allowed = jnp.logical_and(column_ref[rows, :] == row_ref[:, :seen], jnp.logical_not(later))
    bias = jnp.where(allowed, 0.0, -jnp.inf)
    bias = jnp.concatenate([bias] * group)
    for head in range(kv_cols // HEAD_DIM):
        cols = slice(head * HEAD_DIM, (head + 1) * HEAD_DIM)
        base = head * group * HEAD_DIM
        queries = jnp.concatenate([rotated(base + g * HEAD_DIM) for g in range(group)])
        scores = lax.dot_general(
            queries,
            kv_ref[0, :seen, cols],
            (((1,), (1,)), ((), ())),
            preferred_element_type=jnp.float32,
        )
        scores = scores * (1.0 / math.sqrt(HEAD_DIM)) + bias
        expo = jnp.exp(scores - jnp.max(scores, axis=1, keepdims=True))
        weights = (expo * (1.0 / jnp.sum(expo, axis=1, keepdims=True))).astype(jnp.bfloat16)
        mixed = jnp.dot(weights, kv_ref[1, :seen, cols], preferred_element_type=jnp.float32)
        for g in range(group):
            held[:, base + g * HEAD_DIM : base + (g + 1) * HEAD_DIM] = mixed[
                g * size : (g + 1) * size
            ].astype(jnp.bfloat16)
    copy = pltpu.make_async_copy(held, out_ref.at[pl.ds(start, size)], sem)
    copy.start()
    copy.wait()


def attend_piece(start, sums, tables, before, tokens, q_cols):
    size, cols = sums[0].shape
    kv = jax.ShapeDtypeStruct((2, tokens, (cols - q_cols) // 2), jnp.bfloat16)
    out = jax.ShapeDtypeStruct((tokens, q_cols), jnp.bfloat16)
    here = pl.BlockSpec(memory_space=pltpu.VMEM)
    anywhere = pl.BlockSpec(memory_space=pl.ANY)
    return pl.pallas_call(
        functools.partial(attend_kernel, start),
        in_specs=[here] * 8 + ([here, anywhere] if start else []),
        out_specs=[anywhere, here],
        out_shape=[out, kv],
        scratch_shapes=[pltpu.VMEM((size, q_cols), jnp.bfloat16), pltpu.SemaphoreType.DMA],
        input_output_aliases={9: 0} if start else {},
        compiler_params=pltpu.CompilerParams(vmem_limit_bytes=24 * 2**20),
        cost_estimate=pl.CostEstimate(flops=0, bytes_accessed=0, transcendentals=0),
    )(*sums, *tables, *before)


def partial_sums(hidden_states, norm_gain, w_query, w_keyval, segment_ids):
    z = lax.axis_index("fsdp")
    t = lax.axis_index("tensor")
    tokens = hidden_states.shape[0]
    both = ("fsdp", "tensor")
    q_cols = w_query.shape[1]

    def toward(far):
        pairs = []
        for i in range(4):
            for col in range(4):
                j = col if (col // 2 != i // 2) == far else col ^ 2
                pairs.append((i * 4 + col, j * 4 + col // 2 * 2 + ORDER[j].index(i) % 2))
        return pairs

    swap_x = [(n, n ^ 2) for n in range(4)]
    swap_core = [(n, n ^ 1) for n in range(4)]
    outer_in = [(0, 1), (3, 2)]
    count = len(SIZES)

    starts = [sum(SIZES[:n]) * 2 for n in range(count)]
    local_sq = jnp.sum(jnp.square(hidden_states.astype(jnp.float32)), axis=1)
    gain = norm_gain.astype(jnp.float32)
    squares = [
        lax.ppermute(local_sq, "tensor", [(n, n ^ flip) for n in range(4)]) for flip in (1, 3)
    ]
    partner = lax.ppermute(jnp.concatenate((local_sq, gain)), "tensor", swap_x)
    crossed_gain = partner[None, tokens:]
    gain = gain[None, :]

    here_far = t // 2 != z // 2
    even_core = t % 2 == 0
    done = [local_sq]

    def in_turn(*arrays):
        arrays, _ = lax.optimization_barrier((arrays, done[0]))
        return arrays

    state = [{} for _ in SIZES]
    before = ()

    def across(n):
        start, size = starts[n], SIZES[n]
        if n:
            piece = normed[start + size : start + 2 * size]
        else:
            piece = hidden_states[size : 2 * size]
        state[n]["a"] = lax.ppermute(piece, "tensor", swap_x)

    def first_send():
        size = SIZES[0]
        stay, other = in_turn(hidden_states[:size], state[0]["a"])
        far = jnp.where(here_far, stay, other)
        near = jnp.where(here_far, other, stay)
        done[0] = (far, near)
        received = in_turn(partner[:tokens], *squares)
        scale = lax.rsqrt((local_sq + sum(received)) / D + 1e-05)[:, None]

        def scaled(piece, stays):
            row = jnp.where(stays, scale[:size], scale[size : 2 * size])
            col = jnp.where(stays, gain, crossed_gain)
            return (piece.astype(jnp.float32) * row * col).astype(jnp.bfloat16)

        state[0]["s"] = scaled(far, here_far), scaled(near, jnp.logical_not(here_far))
        done[0] = state[0]["s"]
        return (hidden_states.astype(jnp.float32) * scale * gain).astype(jnp.bfloat16)

    def send(n):
        start, size = starts[n], SIZES[n]
        if n:
            stay, other = in_turn(normed[start : start + size], state[n]["a"])
            far = jnp.where(here_far, stay, other)
            near = jnp.where(here_far, other, stay)
            state[n]["s"] = done[0] = (far, near)
        state[n]["z", 0] = lax.ppermute(state[n]["s"][0], both, toward(True))

    def send_near(n):
        (near,) = in_turn(state[n]["s"][1])
        state[n]["z", 1] = lax.ppermute(near, both, toward(False))

    def cross(n, part):
        if n in JOINT:
            mine = jnp.stack(in_turn(state[n]["z", 0], state[n]["z", 1]))
            theirs = lax.ppermute(mine, "tensor", swap_x)
            for half in (0, 1):
                state[n]["x", half] = mine[half], theirs[half]
        else:
            (mine,) = in_turn(state[n]["z", part])
            state[n]["x", part] = mine, lax.ppermute(mine, "tensor", swap_x)
        done[0] = mine

    def both_stages(mine, theirs):
        return jnp.where(even_core, jnp.concatenate((mine, theirs)), jnp.concatenate((theirs, mine)))

    def share(n, part):
        mine, theirs = in_turn(*state[n]["x", part])
        mine = jnp.where(here_far, jnp.concatenate((theirs, mine)), jnp.concatenate((mine, theirs)))
        done[0] = mine
        state[n]["c", part] = mine, lax.ppermute(mine, "tensor", swap_core)

    def multiply(n):
        rows = both_stages(*in_turn(*state[n]["c", 0]))
        outer = jnp.dot(rows, weight, preferred_element_type=jnp.float32).astype(jnp.bfloat16)
        done[0] = outer
        state[n]["p"] = outer, lax.ppermute(outer, "fsdp", outer_in)

    def multiply_near(n):
        rows = both_stages(*in_turn(*state[n]["c", 1]))
        part = jnp.dot(rows, weight, preferred_element_type=jnp.float32)
        size = 2 * SIZES[n]
        inner, state[n]["own"] = part[:size].astype(jnp.bfloat16), part[size:]
        done[0] = inner
        state[n]["e"] = lax.ppermute(inner, "fsdp", [(0, 1), (1, 0), (2, 3), (3, 2)])

    def forward(n):
        outer, passed = in_turn(*state[n]["p"])
        passed = passed + outer
        done[0] = passed
        half = 2 * SIZES[n]
        far_sum = lax.ppermute(passed[:half], "fsdp", [(1, 3), (2, 0)])
        mid_sum = lax.ppermute(passed[half:], "fsdp", [(1, 2), (2, 1)])
        state[n]["f"] = far_sum, mid_sum

    def finish(n):
        added = in_turn(state[n]["own"], state[n]["e"], *state[n]["f"])
        out, kv = attend_piece(starts[n], added, tables, before, tokens, q_cols)
        done[0] = kv
        return kv, out

    seg = segment_ids[0]
    cosine, sine = rope_tables(positions(seg), HEAD_DIM)
    tables = (
        jnp.concatenate((cosine, cosine), 1),
        jnp.concatenate((-sine, sine), 1),
        seg[:, None],
        seg[None, :],
    )
    steps = {
        "a": across,
        "s": send,
        "z": send_near,
        "x": lambda n: cross(n, 0),
        "y": lambda n: cross(n, 1),
        "c": lambda n: share(n, 0),
        "k": lambda n: share(n, 1),
        "m": multiply,
        "e": multiply_near,
        "f": forward,
    }
    for turn in TURNS:
        if turn == "n":
            normed = first_send()
        elif turn == "w":
            w_query, w_keyval = in_turn(w_query, w_keyval)
            weight = jnp.concatenate((w_query, w_keyval.reshape(w_keyval.shape[0], -1)), axis=1)
            done[0] = weight
        elif turn[0] == "d":
            before = finish(int(turn[1]))
        else:
            steps[turn[0]](int(turn[1]))

    return before[1]


def solution(mesh):
    in_specs = (
        P(("groups", "fsdp"), "tensor"),
        P("tensor"),
        P("fsdp", "tensor"),
        P("fsdp", None, "tensor"),
        P(("groups", "fsdp"), None),
    )
    out_specs = P(("groups", "fsdp"), "tensor")
    square = mesh.shape["fsdp"] == 4 and mesh.shape["tensor"] == 4
    step = partial_sums if square else gathered
    return jax.shard_map(step, mesh=mesh, in_specs=in_specs, out_specs=out_specs, check_vma=False)
```

```python
import functools
import math

import jax
import jax.numpy as jnp
from jax import lax
from jax.experimental import pallas as pl
from jax.experimental.pallas import tpu as pltpu
from jax.sharding import PartitionSpec as P

D = 8192
HEAD_DIM = 128
ORDER = ((3, 2, 1, 0), (3, 2, 0, 1), (0, 1, 3, 2), (0, 1, 2, 3))
SIZES = (48, 48, 48, 48)
FAR = ((0,), (1,), (2, 3))
NEAR = ((0, 1), (2, 3))
TURNS = (
    "a0",
    "n",
    "s0",
    "a1",
    "s1",
    "z0",
    "a2",
    "x0",
    "x1",
    "s2",
    "c0",
    "w",
    "z1",
    "y0",
    "c1",
    "m0",
    "k0",
    "x2",
    "m1",
    "f0",
    "e0",
    "c2",
    "m2",
    "y1",
    "e1",
    "f1",
    "d0",
    "k1",
    "f2",
    "m3",
    "e2",
    "d1",
    "e3",
    "f3",
    "d2",
    "d3",
)


def positions(seg):
    length = seg.shape[0]
    index = jnp.arange(length, dtype=jnp.int32)
    change = jnp.concatenate((jnp.ones((1,), dtype=bool), seg[1:] != seg[:-1]))
    first = lax.cummax(jnp.where(change, index, jnp.int32(0)), axis=0)
    return index - first


def rope_tables(place, head_dim):
    half = head_dim // 2
    freq = jnp.exp(jnp.arange(half, dtype=jnp.float32) * (-2.0 * math.log(500000.0) / head_dim))
    angle = place.astype(jnp.float32)[:, None] * freq[None, :]
    return (jnp.cos(angle), jnp.sin(angle))


def rotate(vector, cosine, sine):
    half = vector.shape[-1] // 2
    first = vector[..., :half]
    second = vector[..., half:]
    cosine = cosine[:, None, :]
    sine = sine[:, None, :]
    return jnp.concatenate(
        (first * cosine - second * sine, second * cosine + first * sine), axis=-1
    )


def rotated_keys(keyval, cosine, sine):
    tlen = keyval.shape[0]
    kv_local = keyval.shape[1] // 2
    kv_heads = kv_local // HEAD_DIM
    k_rot = rotate(keyval[:, :kv_local].reshape(tlen, kv_heads, HEAD_DIM), cosine, sine).astype(
        jnp.bfloat16
    )
    v_val = keyval[:, kv_local:].reshape(tlen, kv_heads, HEAD_DIM).astype(jnp.bfloat16)
    return (k_rot, v_val)


def attend(query, k_rot, v_val, seg, cosine, sine, start):
    tlen = query.shape[0]
    klen, kv_heads = k_rot.shape[:2]
    heads = query.shape[1] // HEAD_DIM
    group = heads // kv_heads
    rows = slice(start, start + tlen)
    q_rot = rotate(query.reshape(tlen, heads, HEAD_DIM), cosine[rows], sine[rows]).astype(jnp.bfloat16)
    grouped = q_rot.reshape(tlen, kv_heads, group, HEAD_DIM)
    scores = jnp.einsum("qkgd,skd->kgqs", grouped, k_rot, preferred_element_type=jnp.float32) * (
        1.0 / math.sqrt(HEAD_DIM)
    )
    index = jnp.arange(seg.shape[0], dtype=jnp.int32)
    allowed = (seg[rows, None] == seg[None, :klen]) & (index[None, :klen] <= index[rows, None])
    scores = jnp.where(allowed[None, None], scores, -jnp.inf)
    top = jnp.max(scores, axis=-1, keepdims=True)
    expo = jnp.exp(scores - top)
    weights = (expo / jnp.sum(expo, axis=-1, keepdims=True)).astype(jnp.bfloat16)
    mixed = jnp.einsum("kgqs,skd->qkgd", weights, v_val, preferred_element_type=jnp.float32)
    return mixed.astype(jnp.bfloat16).reshape(tlen, heads * HEAD_DIM)


def gathered(hidden_states, norm_gain, w_query, w_keyval, segment_ids):
    whole = lax.all_gather(hidden_states, "tensor", axis=1, tiled=True)
    gain_full = lax.all_gather(norm_gain, "tensor", axis=0, tiled=True)
    local_sq = jnp.sum(jnp.square(hidden_states.astype(jnp.float32)), axis=1, keepdims=True)
    scale = lax.rsqrt(lax.psum(local_sq, "tensor") / D + 1e-05)
    normed = (whole.astype(jnp.float32) * scale * gain_full.astype(jnp.float32)[None, :]).astype(
        jnp.bfloat16
    )
    w_rows = w_keyval.shape[0]
    kv_weight = w_keyval.reshape(w_rows, 2 * w_keyval.shape[2])
    seg = segment_ids[0]
    cosine, sine = rope_tables(positions(seg), HEAD_DIM)

    def add_rows(piece):
        return jnp.dot(normed, piece, preferred_element_type=jnp.float32)

    query = add_rows(lax.all_gather(w_query, "fsdp", axis=0, tiled=True))
    keyval = add_rows(lax.all_gather(kv_weight, "fsdp", axis=0, tiled=True))
    k_rot, v_val = rotated_keys(keyval, cosine, sine)
    return attend(query, k_rot, v_val, seg, cosine, sine, 0)


def attend_kernel(start, *refs):
    own_ref, near_ref, far_ref, mid_ref, cos_ref, sin_ref, column_ref, row_ref, *refs = refs
    if start:
        old_ref, _, out_ref, kv_ref, held, sem = refs
        kv_ref[...] = old_ref[...]
    else:
        out_ref, kv_ref, held, sem = refs
        kv_ref[...] = jnp.zeros_like(kv_ref)
    size = own_ref.shape[0]
    q_cols = held.shape[1]
    kv_cols = kv_ref.shape[2]
    group = q_cols // kv_cols
    rows = slice(start, start + size)
    seen = min(-(-(start + size) // HEAD_DIM) * HEAD_DIM, kv_ref.shape[1])
    cosine, sine = cos_ref[rows, :], sin_ref[rows, :]

    def total(col):
        cols = slice(col, col + HEAD_DIM)
        return (
            own_ref[:, cols]
            + near_ref[:, cols].astype(jnp.float32)
            + far_ref[:, cols].astype(jnp.float32)
            + mid_ref[:, cols].astype(jnp.float32)
        )

    def rotated(col):
        head = total(col)
        return (head * cosine + pltpu.roll(head, HEAD_DIM // 2, 1) * sine).astype(jnp.bfloat16)

    for col in range(0, kv_cols, HEAD_DIM):
        kv_ref[0, rows, col : col + HEAD_DIM] = rotated(q_cols + col)
        kv_ref[1, rows, col : col + HEAD_DIM] = total(q_cols + kv_cols + col).astype(jnp.bfloat16)
    shape = (size, seen)
    later = lax.broadcasted_iota(jnp.int32, shape, 1) > lax.broadcasted_iota(jnp.int32, shape, 0) + start
    allowed = jnp.logical_and(column_ref[rows, :] == row_ref[:, :seen], jnp.logical_not(later))
    bias = jnp.where(allowed, 0.0, -jnp.inf)
    bias = jnp.concatenate([bias] * group)
    for head in range(kv_cols // HEAD_DIM):
        cols = slice(head * HEAD_DIM, (head + 1) * HEAD_DIM)
        base = head * group * HEAD_DIM
        queries = jnp.concatenate([rotated(base + g * HEAD_DIM) for g in range(group)])
        scores = lax.dot_general(
            queries,
            kv_ref[0, :seen, cols],
            (((1,), (1,)), ((), ())),
            preferred_element_type=jnp.float32,
        )
        scores = scores * (1.0 / math.sqrt(HEAD_DIM)) + bias
        expo = jnp.exp(scores - jnp.max(scores, axis=1, keepdims=True))
        weights = (expo * (1.0 / jnp.sum(expo, axis=1, keepdims=True))).astype(jnp.bfloat16)
        mixed = jnp.dot(weights, kv_ref[1, :seen, cols], preferred_element_type=jnp.float32)
        for g in range(group):
            held[:, base + g * HEAD_DIM : base + (g + 1) * HEAD_DIM] = mixed[
                g * size : (g + 1) * size
            ].astype(jnp.bfloat16)
    copy = pltpu.make_async_copy(held, out_ref.at[pl.ds(start, size)], sem)
    copy.start()
    copy.wait()


def attend_piece(start, sums, tables, before, tokens, q_cols):
    size, cols = sums[0].shape
    kv = jax.ShapeDtypeStruct((2, tokens, (cols - q_cols) // 2), jnp.bfloat16)
    out = jax.ShapeDtypeStruct((tokens, q_cols), jnp.bfloat16)
    here = pl.BlockSpec(memory_space=pltpu.VMEM)
    anywhere = pl.BlockSpec(memory_space=pl.ANY)
    return pl.pallas_call(
        functools.partial(attend_kernel, start),
        in_specs=[here] * 8 + ([here, anywhere] if start else []),
        out_specs=[anywhere, here],
        out_shape=[out, kv],
        scratch_shapes=[pltpu.VMEM((size, q_cols), jnp.bfloat16), pltpu.SemaphoreType.DMA],
        input_output_aliases={9: 0} if start else {},
        compiler_params=pltpu.CompilerParams(vmem_limit_bytes=24 * 2**20),
        cost_estimate=pl.CostEstimate(flops=0, bytes_accessed=0, transcendentals=0),
    )(*sums, *tables, *before)


def partial_sums(hidden_states, norm_gain, w_query, w_keyval, segment_ids):
    z = lax.axis_index("fsdp")
    t = lax.axis_index("tensor")
    tokens = hidden_states.shape[0]
    both = ("fsdp", "tensor")
    q_cols = w_query.shape[1]

    def toward(far):
        pairs = []
        for i in range(4):
            for col in range(4):
                j = col if (col // 2 != i // 2) == far else col ^ 2
                pairs.append((i * 4 + col, j * 4 + col // 2 * 2 + ORDER[j].index(i) % 2))
        return pairs

    swap_x = [(n, n ^ 2) for n in range(4)]
    swap_core = [(n, n ^ 1) for n in range(4)]
    outer_in = [(0, 1), (3, 2)]
    count = len(SIZES)

    starts = [sum(SIZES[:n]) * 2 for n in range(count)]
    local_sq = jnp.sum(jnp.square(hidden_states.astype(jnp.float32)), axis=1)
    gain = norm_gain.astype(jnp.float32)
    squares = [
        lax.ppermute(local_sq, "tensor", [(n, n ^ flip) for n in range(4)]) for flip in (1, 3)
    ]
    partner = lax.ppermute(jnp.concatenate((local_sq, gain)), "tensor", swap_x)
    crossed_gain = partner[None, tokens:]
    gain = gain[None, :]

    here_far = t // 2 != z // 2
    even_core = t % 2 == 0
    done = [local_sq]

    def in_turn(*arrays):
        arrays, _ = lax.optimization_barrier((arrays, done[0]))
        return arrays

    state = [{} for _ in SIZES]
    moved = {}
    before = ()

    stays = [slice(start, start + size) for start, size in zip(starts, SIZES)]
    leaves = [slice(start + size, start + 2 * size) for start, size in zip(starts, SIZES)]

    def joined(pieces):
        return jnp.concatenate(pieces) if len(pieces) > 1 else pieces[0]

    def cut(array, group):
        ends = [sum(SIZES[m] for m in group[: i + 1]) for i in range(len(group))]
        return [array[end - SIZES[m] : end] for m, end in zip(group, ends)]

    def across(g):
        rows = normed if g else hidden_states
        got = lax.ppermute(joined([rows[leaves[n]] for n in FAR[g]]), "tensor", swap_x)
        for n, piece in zip(FAR[g], cut(got, FAR[g])):
            state[n]["a"] = piece

    def first_send():
        size = SIZES[0]
        stay, other = in_turn(hidden_states[:size], state[0]["a"])
        far = jnp.where(here_far, stay, other)
        near = jnp.where(here_far, other, stay)
        done[0] = (far, near)
        received = in_turn(partner[:tokens], *squares)
        scale = lax.rsqrt((local_sq + sum(received)) / D + 1e-05)[:, None]

        def scaled(piece, stays):
            row = jnp.where(stays, scale[:size], scale[size : 2 * size])
            col = jnp.where(stays, gain, crossed_gain)
            return (piece.astype(jnp.float32) * row * col).astype(jnp.bfloat16)

        state[0]["s"] = scaled(far, here_far), scaled(near, jnp.logical_not(here_far))
        done[0] = state[0]["s"]
        return (hidden_states.astype(jnp.float32) * scale * gain).astype(jnp.bfloat16)

    def send(g):
        if g:
            group = FAR[g]
            stay, other = in_turn(
                joined([normed[stays[n]] for n in group]), joined([state[n]["a"] for n in group])
            )
            far = jnp.where(here_far, stay, other)
            near = jnp.where(here_far, other, stay)
            done[0] = (far, near)
            for n, one, two in zip(group, cut(far, group), cut(near, group)):
                state[n]["s"] = one, two
        else:
            far = state[0]["s"][0]
        moved[0, g] = lax.ppermute(far, both, toward(True))

    def send_near(g):
        (near,) = in_turn(joined([state[n]["s"][1] for n in NEAR[g]]))
        done[0] = near
        moved[1, g] = lax.ppermute(near, both, toward(False))

    def cross(part, g):
        (mine,) = in_turn(moved[part, g])
        done[0] = mine
        moved[part, g] = mine, lax.ppermute(mine, "tensor", swap_x)

    def both_stages(mine, theirs):
        return jnp.where(even_core, jnp.concatenate((mine, theirs)), jnp.concatenate((theirs, mine)))

    def share(part, g):
        group = (FAR, NEAR)[part][g]
        mine, theirs = in_turn(*moved[part, g])
        one, two = jnp.where(here_far, theirs, mine), jnp.where(here_far, mine, theirs)
        mine = jnp.concatenate([x for pair in zip(cut(one, group), cut(two, group)) for x in pair])
        done[0] = mine
        theirs = lax.ppermute(mine, "tensor", swap_core)
        first = starts[group[0]]
        for n in group:
            rows = slice(starts[n] - first, starts[n] - first + 2 * SIZES[n])
            state[n]["c", part] = mine[rows], theirs[rows]

    def multiply(n):
        rows = both_stages(*in_turn(*state[n]["c", 0]))
        outer = jnp.dot(rows, weight, preferred_element_type=jnp.float32).astype(jnp.bfloat16)
        done[0] = outer
        state[n]["p"] = outer, lax.ppermute(outer, "fsdp", outer_in)

    def multiply_near(n):
        rows = both_stages(*in_turn(*state[n]["c", 1]))
        part = jnp.dot(rows, weight, preferred_element_type=jnp.float32)
        size = 2 * SIZES[n]
        inner, state[n]["own"] = part[:size].astype(jnp.bfloat16), part[size:]
        done[0] = inner
        state[n]["e"] = lax.ppermute(inner, "fsdp", [(0, 1), (1, 0), (2, 3), (3, 2)])

    def forward(n):
        outer, passed = in_turn(*state[n]["p"])
        passed = passed + outer
        done[0] = passed
        half = 2 * SIZES[n]
        far_sum = lax.ppermute(passed[:half], "fsdp", [(1, 3), (2, 0)])
        mid_sum = lax.ppermute(passed[half:], "fsdp", [(1, 2), (2, 1)])
        state[n]["f"] = far_sum, mid_sum

    def finish(n):
        added = in_turn(state[n]["own"], state[n]["e"], *state[n]["f"])
        out, kv = attend_piece(starts[n], added, tables, before, tokens, q_cols)
        done[0] = kv
        return kv, out

    seg = segment_ids[0]
    cosine, sine = rope_tables(positions(seg), HEAD_DIM)
    tables = (
        jnp.concatenate((cosine, cosine), 1),
        jnp.concatenate((-sine, sine), 1),
        seg[:, None],
        seg[None, :],
    )
    steps = {
        "a": across,
        "s": send,
        "z": send_near,
        "x": functools.partial(cross, 0),
        "y": functools.partial(cross, 1),
        "c": functools.partial(share, 0),
        "k": functools.partial(share, 1),
        "m": multiply,
        "e": multiply_near,
        "f": forward,
    }
    for turn in TURNS:
        if turn == "n":
            normed = first_send()
        elif turn == "w":
            w_query, w_keyval = in_turn(w_query, w_keyval)
            weight = jnp.concatenate((w_query, w_keyval.reshape(w_keyval.shape[0], -1)), axis=1)
            done[0] = weight
        elif turn[0] == "d":
            before = finish(int(turn[1]))
        else:
            steps[turn[0]](int(turn[1]))

    return before[1]


def solution(mesh):
    in_specs = (
        P(("groups", "fsdp"), "tensor"),
        P("tensor"),
        P("fsdp", "tensor"),
        P("fsdp", None, "tensor"),
        P(("groups", "fsdp"), None),
    )
    out_specs = P(("groups", "fsdp"), "tensor")
    square = mesh.shape["fsdp"] == 4 and mesh.shape["tensor"] == 4
    step = partial_sums if square else gathered
    return jax.shard_map(step, mesh=mesh, in_specs=in_specs, out_specs=out_specs, check_vma=False)
```

```python
import functools
import math

import jax
import jax.numpy as jnp
from jax import lax
from jax.experimental import pallas as pl
from jax.experimental.pallas import tpu as pltpu
from jax.sharding import PartitionSpec as P

D = 8192
HEAD_DIM = 128
ORDER = ((3, 2, 1, 0), (3, 2, 0, 1), (0, 1, 3, 2), (0, 1, 2, 3))
SIZES = (48, 48, 48, 48)
FAR = ((0,), (1,), (2, 3))
NEAR = ((0, 1), (2, 3))
TURNS = (
    "a0",
    "n",
    "s0",
    "a1",
    "s1",
    "z0",
    "a2",
    "x0",
    "x1",
    "s2",
    "c0",
    "w",
    "z1",
    "y0",
    "m0",
    "c1",
    "k0",
    "x2",
    "m1",
    "f0",
    "e0",
    "c2",
    "m2",
    "y1",
    "e1",
    "f1",
    "d0",
    "k1",
    "f2",
    "m3",
    "e2",
    "e3",
    "d1",
    "f3",
    "d2",
    "d3",
)


def positions(seg):
    length = seg.shape[0]
    index = jnp.arange(length, dtype=jnp.int32)
    change = jnp.concatenate((jnp.ones((1,), dtype=bool), seg[1:] != seg[:-1]))
    first = lax.cummax(jnp.where(change, index, jnp.int32(0)), axis=0)
    return index - first


def rope_tables(place, head_dim):
    half = head_dim // 2
    freq = jnp.exp(jnp.arange(half, dtype=jnp.float32) * (-2.0 * math.log(500000.0) / head_dim))
    angle = place.astype(jnp.float32)[:, None] * freq[None, :]
    return (jnp.cos(angle), jnp.sin(angle))


def rotate(vector, cosine, sine):
    half = vector.shape[-1] // 2
    first = vector[..., :half]
    second = vector[..., half:]
    cosine = cosine[:, None, :]
    sine = sine[:, None, :]
    return jnp.concatenate(
        (first * cosine - second * sine, second * cosine + first * sine), axis=-1
    )


def rotated_keys(keyval, cosine, sine):
    tlen = keyval.shape[0]
    kv_local = keyval.shape[1] // 2
    kv_heads = kv_local // HEAD_DIM
    k_rot = rotate(keyval[:, :kv_local].reshape(tlen, kv_heads, HEAD_DIM), cosine, sine).astype(
        jnp.bfloat16
    )
    v_val = keyval[:, kv_local:].reshape(tlen, kv_heads, HEAD_DIM).astype(jnp.bfloat16)
    return (k_rot, v_val)


def attend(query, k_rot, v_val, seg, cosine, sine, start):
    tlen = query.shape[0]
    klen, kv_heads = k_rot.shape[:2]
    heads = query.shape[1] // HEAD_DIM
    group = heads // kv_heads
    rows = slice(start, start + tlen)
    q_rot = rotate(query.reshape(tlen, heads, HEAD_DIM), cosine[rows], sine[rows]).astype(jnp.bfloat16)
    grouped = q_rot.reshape(tlen, kv_heads, group, HEAD_DIM)
    scores = jnp.einsum("qkgd,skd->kgqs", grouped, k_rot, preferred_element_type=jnp.float32) * (
        1.0 / math.sqrt(HEAD_DIM)
    )
    index = jnp.arange(seg.shape[0], dtype=jnp.int32)
    allowed = (seg[rows, None] == seg[None, :klen]) & (index[None, :klen] <= index[rows, None])
    scores = jnp.where(allowed[None, None], scores, -jnp.inf)
    top = jnp.max(scores, axis=-1, keepdims=True)
    expo = jnp.exp(scores - top)
    weights = (expo / jnp.sum(expo, axis=-1, keepdims=True)).astype(jnp.bfloat16)
    mixed = jnp.einsum("kgqs,skd->qkgd", weights, v_val, preferred_element_type=jnp.float32)
    return mixed.astype(jnp.bfloat16).reshape(tlen, heads * HEAD_DIM)


def gathered(hidden_states, norm_gain, w_query, w_keyval, segment_ids):
    whole = lax.all_gather(hidden_states, "tensor", axis=1, tiled=True)
    gain_full = lax.all_gather(norm_gain, "tensor", axis=0, tiled=True)
    local_sq = jnp.sum(jnp.square(hidden_states.astype(jnp.float32)), axis=1, keepdims=True)
    scale = lax.rsqrt(lax.psum(local_sq, "tensor") / D + 1e-05)
    normed = (whole.astype(jnp.float32) * scale * gain_full.astype(jnp.float32)[None, :]).astype(
        jnp.bfloat16
    )
    w_rows = w_keyval.shape[0]
    kv_weight = w_keyval.reshape(w_rows, 2 * w_keyval.shape[2])
    seg = segment_ids[0]
    cosine, sine = rope_tables(positions(seg), HEAD_DIM)

    def add_rows(piece):
        return jnp.dot(normed, piece, preferred_element_type=jnp.float32)

    query = add_rows(lax.all_gather(w_query, "fsdp", axis=0, tiled=True))
    keyval = add_rows(lax.all_gather(kv_weight, "fsdp", axis=0, tiled=True))
    k_rot, v_val = rotated_keys(keyval, cosine, sine)
    return attend(query, k_rot, v_val, seg, cosine, sine, 0)


def attend_kernel(start, *refs):
    own_ref, near_ref, far_ref, mid_ref, cos_ref, sin_ref, column_ref, row_ref, *refs = refs
    if start:
        old_ref, _, out_ref, kv_ref, held, sem = refs
        kv_ref[...] = old_ref[...]
    else:
        out_ref, kv_ref, held, sem = refs
        kv_ref[...] = jnp.zeros_like(kv_ref)
    size = own_ref.shape[0]
    q_cols = held.shape[1]
    kv_cols = kv_ref.shape[2]
    group = q_cols // kv_cols
    rows = slice(start, start + size)
    seen = min(-(-(start + size) // HEAD_DIM) * HEAD_DIM, kv_ref.shape[1])
    cosine, sine = cos_ref[rows, :], sin_ref[rows, :]

    def total(col):
        cols = slice(col, col + HEAD_DIM)
        return (
            own_ref[:, cols]
            + near_ref[:, cols].astype(jnp.float32)
            + far_ref[:, cols].astype(jnp.float32)
            + mid_ref[:, cols].astype(jnp.float32)
        )

    def rotated(col):
        head = total(col)
        return (head * cosine + pltpu.roll(head, HEAD_DIM // 2, 1) * sine).astype(jnp.bfloat16)

    for col in range(0, kv_cols, HEAD_DIM):
        kv_ref[0, rows, col : col + HEAD_DIM] = rotated(q_cols + col)
        kv_ref[1, rows, col : col + HEAD_DIM] = total(q_cols + kv_cols + col).astype(jnp.bfloat16)
    shape = (size, seen)
    later = lax.broadcasted_iota(jnp.int32, shape, 1) > lax.broadcasted_iota(jnp.int32, shape, 0) + start
    allowed = jnp.logical_and(column_ref[rows, :] == row_ref[:, :seen], jnp.logical_not(later))
    bias = jnp.where(allowed, 0.0, -jnp.inf)
    bias = jnp.concatenate([bias] * group)
    for head in range(kv_cols // HEAD_DIM):
        cols = slice(head * HEAD_DIM, (head + 1) * HEAD_DIM)
        base = head * group * HEAD_DIM
        queries = jnp.concatenate([rotated(base + g * HEAD_DIM) for g in range(group)])
        scores = lax.dot_general(
            queries,
            kv_ref[0, :seen, cols],
            (((1,), (1,)), ((), ())),
            preferred_element_type=jnp.float32,
        )
        scores = jnp.where(bias < 0, bias, scores * (1.0 / math.sqrt(HEAD_DIM)))
        expo = jnp.exp(scores - jnp.max(scores, axis=1, keepdims=True))
        weights = (expo * (1.0 / jnp.sum(expo, axis=1, keepdims=True))).astype(jnp.bfloat16)
        mixed = jnp.dot(weights, kv_ref[1, :seen, cols], preferred_element_type=jnp.float32)
        for g in range(group):
            held[:, base + g * HEAD_DIM : base + (g + 1) * HEAD_DIM] = mixed[
                g * size : (g + 1) * size
            ].astype(jnp.bfloat16)
    copy = pltpu.make_async_copy(held, out_ref.at[pl.ds(start, size)], sem)
    copy.start()
    copy.wait()


def attend_piece(start, sums, tables, before, tokens, q_cols):
    size, cols = sums[0].shape
    kv = jax.ShapeDtypeStruct((2, tokens, (cols - q_cols) // 2), jnp.bfloat16)
    out = jax.ShapeDtypeStruct((tokens, q_cols), jnp.bfloat16)
    here = pl.BlockSpec(memory_space=pltpu.VMEM)
    anywhere = pl.BlockSpec(memory_space=pl.ANY)
    return pl.pallas_call(
        functools.partial(attend_kernel, start),
        in_specs=[here] * 8 + ([here, anywhere] if start else []),
        out_specs=[anywhere, here],
        out_shape=[out, kv],
        scratch_shapes=[pltpu.VMEM((size, q_cols), jnp.bfloat16), pltpu.SemaphoreType.DMA],
        input_output_aliases={9: 0} if start else {},
        compiler_params=pltpu.CompilerParams(vmem_limit_bytes=24 * 2**20),
        cost_estimate=pl.CostEstimate(flops=0, bytes_accessed=0, transcendentals=0),
    )(*sums, *tables, *before)


def partial_sums(hidden_states, norm_gain, w_query, w_keyval, segment_ids):
    z = lax.axis_index("fsdp")
    t = lax.axis_index("tensor")
    tokens = hidden_states.shape[0]
    both = ("fsdp", "tensor")
    q_cols = w_query.shape[1]

    def toward(far):
        pairs = []
        for i in range(4):
            for col in range(4):
                j = col if (col // 2 != i // 2) == far else col ^ 2
                pairs.append((i * 4 + col, j * 4 + col // 2 * 2 + ORDER[j].index(i) % 2))
        return pairs

    swap_x = [(n, n ^ 2) for n in range(4)]
    swap_core = [(n, n ^ 1) for n in range(4)]
    outer_in = [(0, 1), (3, 2)]
    count = len(SIZES)

    starts = [sum(SIZES[:n]) * 2 for n in range(count)]
    local_sq = jnp.sum(jnp.square(hidden_states.astype(jnp.float32)), axis=1)
    gain = norm_gain.astype(jnp.float32)
    squares = [
        lax.ppermute(local_sq, "tensor", [(n, n ^ flip) for n in range(4)]) for flip in (1, 3)
    ]
    partner = lax.ppermute(jnp.concatenate((local_sq, gain)), "tensor", swap_x)
    crossed_gain = partner[None, tokens:]
    gain = gain[None, :]

    here_far = t // 2 != z // 2
    even_core = t % 2 == 0
    done = [local_sq]

    def in_turn(*arrays):
        arrays, _ = lax.optimization_barrier((arrays, done[0]))
        return arrays

    state = [{} for _ in SIZES]
    moved = {}
    before = ()

    stays = [slice(start, start + size) for start, size in zip(starts, SIZES)]
    leaves = [slice(start + size, start + 2 * size) for start, size in zip(starts, SIZES)]

    def joined(pieces):
        return jnp.concatenate(pieces) if len(pieces) > 1 else pieces[0]

    def cut(array, group):
        ends = [sum(SIZES[m] for m in group[: i + 1]) for i in range(len(group))]
        return [array[end - SIZES[m] : end] for m, end in zip(group, ends)]

    def across(g):
        rows = normed if g else hidden_states
        got = lax.ppermute(joined([rows[leaves[n]] for n in FAR[g]]), "tensor", swap_x)
        for n, piece in zip(FAR[g], cut(got, FAR[g])):
            state[n]["a"] = piece

    def first_send():
        size = SIZES[0]
        stay, other = in_turn(hidden_states[:size], state[0]["a"])
        far = jnp.where(here_far, stay, other)
        near = jnp.where(here_far, other, stay)
        done[0] = (far, near)
        received = in_turn(partner[:tokens], *squares)
        scale = lax.rsqrt((local_sq + sum(received)) / D + 1e-05)[:, None]

        def scaled(piece, stays):
            row = jnp.where(stays, scale[:size], scale[size : 2 * size])
            col = jnp.where(stays, gain, crossed_gain)
            return (piece.astype(jnp.float32) * row * col).astype(jnp.bfloat16)

        state[0]["s"] = scaled(far, here_far), scaled(near, jnp.logical_not(here_far))
        done[0] = state[0]["s"]
        return (hidden_states.astype(jnp.float32) * scale * gain).astype(jnp.bfloat16)

    def send(g):
        if g:
            group = FAR[g]
            stay, other = in_turn(
                joined([normed[stays[n]] for n in group]), joined([state[n]["a"] for n in group])
            )
            far = jnp.where(here_far, stay, other)
            near = jnp.where(here_far, other, stay)
            done[0] = (far, near)
            for n, one, two in zip(group, cut(far, group), cut(near, group)):
                state[n]["s"] = one, two
        else:
            far = state[0]["s"][0]
        moved[0, g] = lax.ppermute(far, both, toward(True))

    def send_near(g):
        (near,) = in_turn(joined([state[n]["s"][1] for n in NEAR[g]]))
        done[0] = near
        moved[1, g] = lax.ppermute(near, both, toward(False))

    def cross(part, g):
        (mine,) = in_turn(moved[part, g])
        done[0] = mine
        moved[part, g] = mine, lax.ppermute(mine, "tensor", swap_x)

    def both_stages(mine, theirs):
        return jnp.where(even_core, jnp.concatenate((mine, theirs)), jnp.concatenate((theirs, mine)))

    def share(part, g):
        group = (FAR, NEAR)[part][g]
        mine, theirs = in_turn(*moved[part, g])
        one, two = jnp.where(here_far, theirs, mine), jnp.where(here_far, mine, theirs)
        mine = jnp.concatenate([x for pair in zip(cut(one, group), cut(two, group)) for x in pair])
        done[0] = mine
        theirs = lax.ppermute(mine, "tensor", swap_core)
        first = starts[group[0]]
        for n in group:
            rows = slice(starts[n] - first, starts[n] - first + 2 * SIZES[n])
            state[n]["c", part] = mine[rows], theirs[rows]

    def multiply(n):
        rows = both_stages(*in_turn(*state[n]["c", 0]))
        outer = jnp.dot(rows, weight, preferred_element_type=jnp.float32).astype(jnp.bfloat16)
        done[0] = outer
        state[n]["p"] = outer, lax.ppermute(outer, "fsdp", outer_in)

    def multiply_near(n):
        rows = both_stages(*in_turn(*state[n]["c", 1]))
        part = jnp.dot(rows, weight, preferred_element_type=jnp.float32)
        size = 2 * SIZES[n]
        inner, state[n]["own"] = part[:size].astype(jnp.bfloat16), part[size:]
        done[0] = inner
        state[n]["e"] = lax.ppermute(inner, "fsdp", [(0, 1), (1, 0), (2, 3), (3, 2)])

    def forward(n):
        outer, passed = in_turn(*state[n]["p"])
        passed = passed + outer
        done[0] = passed
        half = 2 * SIZES[n]
        far_sum = lax.ppermute(passed[:half], "fsdp", [(1, 3), (2, 0)])
        mid_sum = lax.ppermute(passed[half:], "fsdp", [(1, 2), (2, 1)])
        state[n]["f"] = far_sum, mid_sum

    def finish(n):
        added = in_turn(state[n]["own"], state[n]["e"], *state[n]["f"])
        out, kv = attend_piece(starts[n], added, tables, before, tokens, q_cols)
        done[0] = kv
        return kv, out

    seg = segment_ids[0]
    cosine, sine = rope_tables(positions(seg), HEAD_DIM)
    tables = (
        jnp.concatenate((cosine, cosine), 1),
        jnp.concatenate((-sine, sine), 1),
        seg[:, None],
        seg[None, :],
    )
    steps = {
        "a": across,
        "s": send,
        "z": send_near,
        "x": functools.partial(cross, 0),
        "y": functools.partial(cross, 1),
        "c": functools.partial(share, 0),
        "k": functools.partial(share, 1),
        "m": multiply,
        "e": multiply_near,
        "f": forward,
    }
    for turn in TURNS:
        if turn == "n":
            normed = first_send()
        elif turn == "w":
            w_query, w_keyval = in_turn(w_query, w_keyval)
            weight = jnp.concatenate((w_query, w_keyval.reshape(w_keyval.shape[0], -1)), axis=1)
            done[0] = weight
        elif turn[0] == "d":
            before = finish(int(turn[1]))
        else:
            steps[turn[0]](int(turn[1]))

    return before[1]


def solution(mesh):
    in_specs = (
        P(("groups", "fsdp"), "tensor"),
        P("tensor"),
        P("fsdp", "tensor"),
        P("fsdp", None, "tensor"),
        P(("groups", "fsdp"), None),
    )
    out_specs = P(("groups", "fsdp"), "tensor")
    square = mesh.shape["fsdp"] == 4 and mesh.shape["tensor"] == 4
    step = partial_sums if square else gathered
    return jax.shard_map(step, mesh=mesh, in_specs=in_specs, out_specs=out_specs, check_vma=False)
```

```python
import functools
import math

import jax
import jax.numpy as jnp
from jax import lax
from jax.experimental import pallas as pl
from jax.experimental.pallas import tpu as pltpu
from jax.sharding import PartitionSpec as P

D = 8192
HEAD_DIM = 128
ORDER = ((3, 2, 1, 0), (3, 2, 0, 1), (0, 1, 3, 2), (0, 1, 2, 3))
SIZES = (48, 64, 48, 32)
FAR = ((0,), (1,), (2, 3))
NEAR = ((0, 1), (2, 3))
TURNS = (
    "a0",
    "n",
    "s0",
    "a2",
    "a1",
    "s1",
    "z0",
    "x0",
    "x1",
    "s2",
    "c0",
    "w",
    "z1",
    "y0",
    "m0",
    "c1",
    "k0",
    "x2",
    "m1",
    "f0",
    "e0",
    "c2",
    "m2",
    "y1",
    "e1",
    "f1",
    "d0",
    "k1",
    "f2",
    "m3",
    "e2",
    "e3",
    "d1",
    "f3",
    "d2",
    "d3",
)


def positions(seg):
    length = seg.shape[0]
    index = jnp.arange(length, dtype=jnp.int32)
    change = jnp.concatenate((jnp.ones((1,), dtype=bool), seg[1:] != seg[:-1]))
    first = lax.cummax(jnp.where(change, index, jnp.int32(0)), axis=0)
    return index - first


def rope_tables(place, head_dim):
    half = head_dim // 2
    freq = jnp.exp(jnp.arange(half, dtype=jnp.float32) * (-2.0 * math.log(500000.0) / head_dim))
    angle = place.astype(jnp.float32)[:, None] * freq[None, :]
    return (jnp.cos(angle), jnp.sin(angle))


def rotate(vector, cosine, sine):
    half = vector.shape[-1] // 2
    first = vector[..., :half]
    second = vector[..., half:]
    cosine = cosine[:, None, :]
    sine = sine[:, None, :]
    return jnp.concatenate(
        (first * cosine - second * sine, second * cosine + first * sine), axis=-1
    )


def rotated_keys(keyval, cosine, sine):
    tlen = keyval.shape[0]
    kv_local = keyval.shape[1] // 2
    kv_heads = kv_local // HEAD_DIM
    k_rot = rotate(keyval[:, :kv_local].reshape(tlen, kv_heads, HEAD_DIM), cosine, sine).astype(
        jnp.bfloat16
    )
    v_val = keyval[:, kv_local:].reshape(tlen, kv_heads, HEAD_DIM).astype(jnp.bfloat16)
    return (k_rot, v_val)


def attend(query, k_rot, v_val, seg, cosine, sine, start):
    tlen = query.shape[0]
    klen, kv_heads = k_rot.shape[:2]
    heads = query.shape[1] // HEAD_DIM
    group = heads // kv_heads
    rows = slice(start, start + tlen)
    q_rot = rotate(query.reshape(tlen, heads, HEAD_DIM), cosine[rows], sine[rows]).astype(jnp.bfloat16)
    grouped = q_rot.reshape(tlen, kv_heads, group, HEAD_DIM)
    scores = jnp.einsum("qkgd,skd->kgqs", grouped, k_rot, preferred_element_type=jnp.float32) * (
        1.0 / math.sqrt(HEAD_DIM)
    )
    index = jnp.arange(seg.shape[0], dtype=jnp.int32)
    allowed = (seg[rows, None] == seg[None, :klen]) & (index[None, :klen] <= index[rows, None])
    scores = jnp.where(allowed[None, None], scores, -jnp.inf)
    top = jnp.max(scores, axis=-1, keepdims=True)
    expo = jnp.exp(scores - top)
    weights = (expo / jnp.sum(expo, axis=-1, keepdims=True)).astype(jnp.bfloat16)
    mixed = jnp.einsum("kgqs,skd->qkgd", weights, v_val, preferred_element_type=jnp.float32)
    return mixed.astype(jnp.bfloat16).reshape(tlen, heads * HEAD_DIM)


def gathered(hidden_states, norm_gain, w_query, w_keyval, segment_ids):
    whole = lax.all_gather(hidden_states, "tensor", axis=1, tiled=True)
    gain_full = lax.all_gather(norm_gain, "tensor", axis=0, tiled=True)
    local_sq = jnp.sum(jnp.square(hidden_states.astype(jnp.float32)), axis=1, keepdims=True)
    scale = lax.rsqrt(lax.psum(local_sq, "tensor") / D + 1e-05)
    normed = (whole.astype(jnp.float32) * scale * gain_full.astype(jnp.float32)[None, :]).astype(
        jnp.bfloat16
    )
    w_rows = w_keyval.shape[0]
    kv_weight = w_keyval.reshape(w_rows, 2 * w_keyval.shape[2])
    seg = segment_ids[0]
    cosine, sine = rope_tables(positions(seg), HEAD_DIM)

    def add_rows(piece):
        return jnp.dot(normed, piece, preferred_element_type=jnp.float32)

    query = add_rows(lax.all_gather(w_query, "fsdp", axis=0, tiled=True))
    keyval = add_rows(lax.all_gather(kv_weight, "fsdp", axis=0, tiled=True))
    k_rot, v_val = rotated_keys(keyval, cosine, sine)
    return attend(query, k_rot, v_val, seg, cosine, sine, 0)


def attend_kernel(start, *refs):
    own_ref, near_ref, far_ref, mid_ref, cos_ref, sin_ref, column_ref, row_ref, *refs = refs
    if start:
        old_ref, _, out_ref, kv_ref, held, sem = refs
        kv_ref[...] = old_ref[...]
    else:
        out_ref, kv_ref, held, sem = refs
        kv_ref[...] = jnp.zeros_like(kv_ref)
    size = own_ref.shape[0]
    q_cols = held.shape[1]
    kv_cols = kv_ref.shape[2]
    group = q_cols // kv_cols
    rows = slice(start, start + size)
    seen = min(-(-(start + size) // HEAD_DIM) * HEAD_DIM, kv_ref.shape[1])
    cosine, sine = cos_ref[rows, :], sin_ref[rows, :]

    def total(col):
        cols = slice(col, col + HEAD_DIM)
        return (
            own_ref[:, cols]
            + near_ref[:, cols].astype(jnp.float32)
            + far_ref[:, cols].astype(jnp.float32)
            + mid_ref[:, cols].astype(jnp.float32)
        )

    def rotated(col):
        head = total(col)
        return (head * cosine + pltpu.roll(head, HEAD_DIM // 2, 1) * sine).astype(jnp.bfloat16)

    for col in range(0, kv_cols, HEAD_DIM):
        kv_ref[0, rows, col : col + HEAD_DIM] = rotated(q_cols + col)
        kv_ref[1, rows, col : col + HEAD_DIM] = total(q_cols + kv_cols + col).astype(jnp.bfloat16)
    shape = (size, seen)
    later = lax.broadcasted_iota(jnp.int32, shape, 1) > lax.broadcasted_iota(jnp.int32, shape, 0) + start
    allowed = jnp.logical_and(column_ref[rows, :] == row_ref[:, :seen], jnp.logical_not(later))
    bias = jnp.where(allowed, 0.0, -jnp.inf)
    bias = jnp.concatenate([bias] * group)
    for head in range(kv_cols // HEAD_DIM):
        cols = slice(head * HEAD_DIM, (head + 1) * HEAD_DIM)
        base = head * group * HEAD_DIM
        queries = jnp.concatenate([rotated(base + g * HEAD_DIM) for g in range(group)])
        scores = lax.dot_general(
            queries,
            kv_ref[0, :seen, cols],
            (((1,), (1,)), ((), ())),
            preferred_element_type=jnp.float32,
        )
        scores = jnp.where(bias < 0, bias, scores * (1.0 / math.sqrt(HEAD_DIM)))
        expo = jnp.exp(scores - jnp.max(scores, axis=1, keepdims=True))
        weights = (expo * (1.0 / jnp.sum(expo, axis=1, keepdims=True))).astype(jnp.bfloat16)
        mixed = jnp.dot(weights, kv_ref[1, :seen, cols], preferred_element_type=jnp.float32)
        for g in range(group):
            held[:, base + g * HEAD_DIM : base + (g + 1) * HEAD_DIM] = mixed[
                g * size : (g + 1) * size
            ].astype(jnp.bfloat16)
    copy = pltpu.make_async_copy(held, out_ref.at[pl.ds(start, size)], sem)
    copy.start()
    copy.wait()


def attend_piece(start, sums, tables, before, tokens, q_cols):
    size, cols = sums[0].shape
    kv = jax.ShapeDtypeStruct((2, tokens, (cols - q_cols) // 2), jnp.bfloat16)
    out = jax.ShapeDtypeStruct((tokens, q_cols), jnp.bfloat16)
    here = pl.BlockSpec(memory_space=pltpu.VMEM)
    anywhere = pl.BlockSpec(memory_space=pl.ANY)
    return pl.pallas_call(
        functools.partial(attend_kernel, start),
        in_specs=[here] * 8 + ([here, anywhere] if start else []),
        out_specs=[anywhere, here],
        out_shape=[out, kv],
        scratch_shapes=[pltpu.VMEM((size, q_cols), jnp.bfloat16), pltpu.SemaphoreType.DMA],
        input_output_aliases={9: 0} if start else {},
        compiler_params=pltpu.CompilerParams(vmem_limit_bytes=24 * 2**20),
        cost_estimate=pl.CostEstimate(flops=0, bytes_accessed=0, transcendentals=0),
    )(*sums, *tables, *before)


def partial_sums(hidden_states, norm_gain, w_query, w_keyval, segment_ids):
    z = lax.axis_index("fsdp")
    t = lax.axis_index("tensor")
    tokens = hidden_states.shape[0]
    both = ("fsdp", "tensor")
    q_cols = w_query.shape[1]

    def toward(far):
        pairs = []
        for i in range(4):
            for col in range(4):
                j = col if (col // 2 != i // 2) == far else col ^ 2
                pairs.append((i * 4 + col, j * 4 + col // 2 * 2 + ORDER[j].index(i) % 2))
        return pairs

    swap_x = [(n, n ^ 2) for n in range(4)]
    swap_core = [(n, n ^ 1) for n in range(4)]
    outer_in = [(0, 1), (3, 2)]
    count = len(SIZES)

    starts = [sum(SIZES[:n]) * 2 for n in range(count)]
    local_sq = jnp.sum(jnp.square(hidden_states.astype(jnp.float32)), axis=1)
    gain = norm_gain.astype(jnp.float32)
    squares = [
        lax.ppermute(local_sq, "tensor", [(n, n ^ flip) for n in range(4)]) for flip in (1, 3)
    ]
    partner = lax.ppermute(jnp.concatenate((local_sq, gain)), "tensor", swap_x)
    crossed_gain = partner[None, tokens:]
    gain = gain[None, :]

    here_far = t // 2 != z // 2
    even_core = t % 2 == 0
    done = [local_sq]

    def in_turn(*arrays):
        arrays, _ = lax.optimization_barrier((arrays, done[0]))
        return arrays

    state = [{} for _ in SIZES]
    moved = {}
    before = ()

    stays = [slice(start, start + size) for start, size in zip(starts, SIZES)]
    leaves = [slice(start + size, start + 2 * size) for start, size in zip(starts, SIZES)]

    def joined(pieces):
        return jnp.concatenate(pieces) if len(pieces) > 1 else pieces[0]

    def cut(array, group):
        ends = [sum(SIZES[m] for m in group[: i + 1]) for i in range(len(group))]
        return [array[end - SIZES[m] : end] for m, end in zip(group, ends)]

    def across(g):
        rows = normed if g else hidden_states
        got = lax.ppermute(joined([rows[leaves[n]] for n in FAR[g]]), "tensor", swap_x)
        for n, piece in zip(FAR[g], cut(got, FAR[g])):
            state[n]["a"] = piece

    def first_send():
        size = SIZES[0]
        stay, other = in_turn(hidden_states[:size], state[0]["a"])
        far = jnp.where(here_far, stay, other)
        near = jnp.where(here_far, other, stay)
        done[0] = (far, near)
        received = in_turn(partner[:tokens], *squares)
        scale = lax.rsqrt((local_sq + sum(received)) / D + 1e-05)[:, None]

        def scaled(piece, stays):
            row = jnp.where(stays, scale[:size], scale[size : 2 * size])
            col = jnp.where(stays, gain, crossed_gain)
            return (piece.astype(jnp.float32) * row * col).astype(jnp.bfloat16)

        state[0]["s"] = scaled(far, here_far), scaled(near, jnp.logical_not(here_far))
        done[0] = state[0]["s"]
        return (hidden_states.astype(jnp.float32) * scale * gain).astype(jnp.bfloat16)

    def send(g):
        if g:
            group = FAR[g]
            stay, other = in_turn(
                joined([normed[stays[n]] for n in group]), joined([state[n]["a"] for n in group])
            )
            far = jnp.where(here_far, stay, other)
            near = jnp.where(here_far, other, stay)
            done[0] = (far, near)
            for n, one, two in zip(group, cut(far, group), cut(near, group)):
                state[n]["s"] = one, two
        else:
            far = state[0]["s"][0]
        moved[0, g] = lax.ppermute(far, both, toward(True))

    def send_near(g):
        (near,) = in_turn(joined([state[n]["s"][1] for n in NEAR[g]]))
        done[0] = near
        moved[1, g] = lax.ppermute(near, both, toward(False))

    def cross(part, g):
        (mine,) = in_turn(moved[part, g])
        done[0] = mine
        moved[part, g] = mine, lax.ppermute(mine, "tensor", swap_x)

    def both_stages(mine, theirs):
        return jnp.where(even_core, jnp.concatenate((mine, theirs)), jnp.concatenate((theirs, mine)))

    def share(part, g):
        group = (FAR, NEAR)[part][g]
        mine, theirs = in_turn(*moved[part, g])
        one, two = jnp.where(here_far, theirs, mine), jnp.where(here_far, mine, theirs)
        mine = jnp.concatenate([x for pair in zip(cut(one, group), cut(two, group)) for x in pair])
        done[0] = mine
        theirs = lax.ppermute(mine, "tensor", swap_core)
        first = starts[group[0]]
        for n in group:
            rows = slice(starts[n] - first, starts[n] - first + 2 * SIZES[n])
            state[n]["c", part] = mine[rows], theirs[rows]

    def multiply(n):
        rows = both_stages(*in_turn(*state[n]["c", 0]))
        outer = jnp.dot(rows, weight, preferred_element_type=jnp.float32).astype(jnp.bfloat16)
        done[0] = outer
        state[n]["p"] = outer, lax.ppermute(outer, "fsdp", outer_in)

    def multiply_near(n):
        rows = both_stages(*in_turn(*state[n]["c", 1]))
        part = jnp.dot(rows, weight, preferred_element_type=jnp.float32)
        size = 2 * SIZES[n]
        inner, state[n]["own"] = part[:size].astype(jnp.bfloat16), part[size:]
        done[0] = inner
        state[n]["e"] = lax.ppermute(inner, "fsdp", [(0, 1), (1, 0), (2, 3), (3, 2)])

    def forward(n):
        outer, passed = in_turn(*state[n]["p"])
        passed = passed + outer
        done[0] = passed
        half = 2 * SIZES[n]
        far_sum = lax.ppermute(passed[:half], "fsdp", [(1, 3), (2, 0)])
        mid_sum = lax.ppermute(passed[half:], "fsdp", [(1, 2), (2, 1)])
        state[n]["f"] = far_sum, mid_sum

    def finish(n):
        added = in_turn(state[n]["own"], state[n]["e"], *state[n]["f"])
        out, kv = attend_piece(starts[n], added, tables, before, tokens, q_cols)
        done[0] = kv
        return kv, out

    seg = segment_ids[0]
    cosine, sine = rope_tables(positions(seg), HEAD_DIM)
    tables = (
        jnp.concatenate((cosine, cosine), 1),
        jnp.concatenate((-sine, sine), 1),
        seg[:, None],
        seg[None, :],
    )
    steps = {
        "a": across,
        "s": send,
        "z": send_near,
        "x": functools.partial(cross, 0),
        "y": functools.partial(cross, 1),
        "c": functools.partial(share, 0),
        "k": functools.partial(share, 1),
        "m": multiply,
        "e": multiply_near,
        "f": forward,
    }
    for turn in TURNS:
        if turn == "n":
            normed = first_send()
        elif turn == "w":
            w_query, w_keyval = in_turn(w_query, w_keyval)
            weight = jnp.concatenate((w_query, w_keyval.reshape(w_keyval.shape[0], -1)), axis=1)
            done[0] = weight
        elif turn[0] == "d":
            before = finish(int(turn[1]))
        else:
            steps[turn[0]](int(turn[1]))

    return before[1]


def solution(mesh):
    in_specs = (
        P(("groups", "fsdp"), "tensor"),
        P("tensor"),
        P("fsdp", "tensor"),
        P("fsdp", None, "tensor"),
        P(("groups", "fsdp"), None),
    )
    out_specs = P(("groups", "fsdp"), "tensor")
    square = mesh.shape["fsdp"] == 4 and mesh.shape["tensor"] == 4
    step = partial_sums if square else gathered
    return jax.shard_map(step, mesh=mesh, in_specs=in_specs, out_specs=out_specs, check_vma=False)
```
